32 devices in a mesh: uly: 2 (over y), blk: 16 (over z, x, core).
Axes of the slice: x: 2, y: 2, z: 4, core: 2. Of those that a mesh axis runs over, the one named last changes fastest.
Arguments:
- query: bfloat16 [8192, 1024], P(('uly', 'blk')), as said below
- key: bfloat16 [8192, 1024], P(('uly', 'blk')), as said below
- value: bfloat16 [8192, 1024], P(('uly', 'blk')), may hold values from -5 to 5
- live: int32 [8, 4, 16, 27], P('uly', None, 'blk'), may hold values from 0 to 1, as said below
Outputs:
- attended: bfloat16 [8192, 1024], P(('uly', 'blk'))
The draws below stay inside these ranges and needn't reach their ends.
Inputs may be any that keep to these rules, and one draw needn't show every extreme that they name: `query`: entries lie within -5 to 5. `key`: entries lie within -5 to 5. live[h, f, s, 13] = 1 always; live is 0 for every neighbour that lies outside the grid of 4 x 2 x 8 tiles.
All inputs are finite; a program needn't handle non-finite values.
Results may differ from the reference program's by a relative error of at most 0.0046.
Values may be sent and summed in bfloat16 or wider, within the bound.
No kernel may reach another device: no remote copies, remote signals or barrier semaphores. Data moves between devices by JAX's collectives and lax.ppermute only.
A program may use at most 128 MiB of HBM per device.

```python
import jax
import jax.numpy as jnp
from jax import lax

HD = 128
HEADS = 8
TILE = 128
TW = 8
TPD = 2
SPATIAL = 16
TH = 2
FRAMES = 4
TOKENS = 8192
N_ULY = 2
N_BLK = 16


def draw_query(key, part):
    own = jax.random.fold_in(key, 11)
    base = jnp.clip(jax.random.normal(own, (TOKENS, HEADS * HD), jnp.float32), -5.0, 5.0)
    return base.astype(jnp.bfloat16)


def draw_key(key, part):
    own = jax.random.fold_in(key, 12)
    base = jnp.clip(jax.random.normal(own, (TOKENS, HEADS * HD), jnp.float32), -5.0, 5.0)
    return base.astype(jnp.bfloat16)


def draw_live(key, part):
    own = jax.random.fold_in(key, 21)
    chance_key, roll_key, reach_key = jax.random.split(own, 3)
    chance = jax.random.randint(chance_key, (HEADS, 1, 1, 1), 30, 91)
    rolls = jax.random.randint(roll_key, (HEADS, FRAMES, SPATIAL, 27), 0, 100)
    reach = jax.random.randint(reach_key, (HEADS, 1, 1, 1), 0, 2)
    offsets = jnp.arange(27)
    frame_step = offsets // 9 - 1
    row_step = offsets // 3 % 3 - 1
    col_step = offsets % 3 - 1
    frames = jnp.arange(FRAMES)[:, None, None]
    spots = jnp.arange(SPATIAL)[None, :, None]
    heights = spots // TW + row_step
    widths = spots % TW + col_step
    inside = (frames + frame_step >= 0) & (frames + frame_step < FRAMES)
    inside = inside & (heights >= 0) & (heights < TH) & (widths >= 0) & (widths < TW)
    chosen = (rolls < chance) & (jnp.abs(frame_step) <= reach)
    keep = inside[None] & ((offsets == 13) | chosen)
    return keep.astype(jnp.int32)


def shard_levels(rng, shape, cuts, low, largest):
    loudness, own = 1.0, jax.random.fold_in(rng, 6)
    for axis_at, blocks in cuts:
        steps = jnp.exp(jax.random.uniform(jax.random.fold_in(own, axis_at), (blocks,), jnp.float32, low / len(cuts), largest / len(cuts)))
        loudness = loudness * jnp.repeat(steps, shape[axis_at] // blocks).reshape([-1 if axis == axis_at else 1 for axis in range(len(shape))])
    return loudness


def centred(key, shape, scale, bound, shards=(), held_as=jnp.bfloat16):
    loudness = shard_levels(key, shape, shards, -0.22, 0.18) if shards else 1.0
    values = jax.random.normal(key, shape, jnp.float32) * scale * loudness
    return jnp.minimum(jnp.maximum(values, -bound), bound).astype(held_as)


def setup_inputs(seed: int = 0) -> dict:
    arg_keys = jax.random.split(jax.random.key(seed), 5)
    return {
        "query": draw_query(jax.random.fold_in(arg_keys[4], 71), 0),
        "key": draw_key(jax.random.fold_in(arg_keys[4], 71), 0),
        "value": centred(arg_keys[2], (TOKENS, HEADS * HD), 1.0, 5.0, ((0, 32),)),
        "live": draw_live(jax.random.fold_in(arg_keys[4], 71), 0),
    }


def reference(query, key, value, live):
    scale = HD ** -0.5

    def tiles(tensor):
        shaped = tensor.reshape(N_ULY, N_BLK, TPD, TILE, HEADS, HD).transpose(4, 0, 2, 1, 3, 5)
        return shaped.reshape(HEADS, FRAMES, TH, TW, TILE, HD)

    grid_pad = ((1, 1), (1, 1), (1, 1), (0, 0), (0, 0))

    def one_head(inputs):
        query_head, key_head, value_head, live_head = inputs
        key_pad = jnp.pad(key_head, grid_pad)
        value_pad = jnp.pad(value_head, grid_pad)
        allowed_head = live_head.reshape(FRAMES, TH, TW, 27)

        def beside_all(block):
            parts = [block[frame_step, row_step:row_step + TH, col_step:col_step + TW]
                     for frame_step in range(3) for row_step in range(3) for col_step in range(3)]
            return jnp.stack(parts, axis=2)

        def one_frame(frame):
            key_near = beside_all(lax.dynamic_slice_in_dim(key_pad, frame, 3, 0)).astype(jnp.float32)
            value_near = beside_all(lax.dynamic_slice_in_dim(value_pad, frame, 3, 0)).astype(jnp.float32)
            query_frame = lax.dynamic_index_in_dim(query_head, frame, 0, keepdims=False).astype(jnp.float32)
            scores = jnp.einsum("abqd,abokd->abqok", query_frame, key_near,
                                precision=lax.Precision.HIGHEST) * scale
            allowed = (lax.dynamic_index_in_dim(allowed_head, frame, 0, keepdims=False) > 0)[:, :, None, :, None]
            masked = jnp.where(allowed, scores, -1e30)
            top = jnp.max(masked, axis=(3, 4), keepdims=True)
            weights = jnp.where(allowed, jnp.exp(masked - top), 0.0)
            total = jnp.sum(weights, axis=(3, 4))
            rounded = lax.optimization_barrier(weights.astype(jnp.bfloat16)).astype(jnp.float32)
            mixed = jnp.einsum("abqok,abokd->abqd", rounded, value_near,
                               precision=lax.Precision.HIGHEST)
            return (mixed / total[..., None]).astype(jnp.bfloat16)

        return lax.map(one_frame, jnp.arange(FRAMES))

    result = lax.map(one_head, (tiles(query), tiles(key), tiles(value), live))
    result = result.reshape(HEADS, N_ULY, TPD, N_BLK, TILE, HD).transpose(1, 3, 2, 4, 0, 5)
    return result.reshape(TOKENS, HEADS * HD)
```

```python
import functools

import jax
import jax.numpy as jnp
from jax import lax
from jax.experimental import pallas as pl
from jax.experimental.pallas import tpu as pltpu
from jax.sharding import PartitionSpec as P

HD = 128
HEADS = 8
TILE = 128
TW = 8
NEAR = 27
STEP = 4
COL = STEP * HD
C2 = HD ** (-0.5) * 1.4426950408889634
NONE = -1e30
VMEM = 63 * 2**20

ANYWHERE = pl.BlockSpec(memory_space=pl.ANY)
IN_SMEM = pl.BlockSpec(memory_space=pltpu.SMEM)
IN_VMEM = pl.BlockSpec(memory_space=pltpu.VMEM)


def frame_of(at):
    if lax.axis_size("uly") == 2:
        g = lax.axis_index("uly")
        return 1 - g if at == 0 else g
    return at


def slots_of(at):
    if lax.axis_size("uly") == 2:
        outward = 1 - 2 * lax.axis_index("uly")
        return ((0, 0), (1, -outward), (2, outward)) if at == 0 else ((0, outward), (1, 0))
    return ((0, 0), (1, 1), (2, -1)) if at == 0 else ((0, -1), (1, 0), (3, 1))


def rows_of(at):
    return pl.ds(pl.multiple_of(frame_of(at) * TILE, TILE), TILE)


def pack_kernel(key, value, first, second, sems):
    copies = []
    for at, out in enumerate((first, second)):
        for part, source in enumerate((key, value)):
            copies.append(
                pltpu.make_async_copy(
                    source.at[rows_of(at)], out.at[pl.ds(part * TILE, TILE)], sems.at[at, part]
                )
            )
    for copy in copies:
        copy.start()
    for copy in copies:
        copy.wait()


def pack(key, value):
    shape = jax.ShapeDtypeStruct((2 * TILE, HEADS * HD), key.dtype)
    return pl.pallas_call(
        pack_kernel,
        out_shape=(shape, shape),
        in_specs=[ANYWHERE, ANYWHERE],
        out_specs=(IN_VMEM, IN_VMEM),
        scratch_shapes=[pltpu.SemaphoreType.DMA((2, 2))],
        compiler_params=pltpu.CompilerParams(vmem_limit_bytes=VMEM),
        cost_estimate=pl.CostEstimate(flops=0, bytes_accessed=2**21, transcendentals=0),
        name="pack_kv",
    )(key, value)


def attend_kernel(at, height_step, n_slots, normalise, live, query, *refs):
    tiles = refs[: 3 * n_slots]
    out, stats_out = refs[-2:]
    step = pl.program_id(0)
    n_uly = lax.axis_size("uly")
    g, s = lax.axis_index("uly"), lax.axis_index("blk")
    height = 2 * (s // TW) - 1 if height_step is None else height_step
    width = 1 - 2 * (s % 2)
    offsets = [
        9 * (frame_step + 1) + 3 * (height + 1) + width_step + 1
        for _, frame_step in slots_of(at)
        for width_step in (0, width, -width)
    ]
    n = len(offsets)
    rows = rows_of(at)

    def live_row(h):
        head = step * STEP + h
        if n_uly == 2:
            held = HEADS // n_uly
            half = lax.rem(lax.div(head, held) + g, 2)
            return (half * held + lax.rem(head, held)) * 4 * NEAR + (2 * g + frame_of(at)) * NEAR
        return head * 2 * NEAR + frame_of(at) * NEAR

    heads = range(STEP)
    cols = [slice(h * HD, (h + 1) * HD) for h in heads]
    scores, highest = {}, {}
    for h in heads:
        row = live_row(h)
        q = query[rows, cols[h]]
        for t in range(n):
            score = lax.dot_general(
                q,
                tiles[t][:TILE, cols[h]],
                (((1,), (1,)), ((), ())),
                preferred_element_type=jnp.float32,
            )
            score = score + jnp.where(live[row + offsets[t]] > 0, 0.0, NONE)
            scores[h, t] = score
            highest[h] = score if t == 0 else jnp.maximum(highest[h], score)
    top = {h: jnp.max(highest[h], axis=1, keepdims=True) for h in heads}
    shift = {h: top[h] * C2 for h in heads}
    mixed, sums = {}, {}
    for h in heads:
        for t in range(n):
            w = jnp.exp2(scores[h, t] * C2 - shift[h])
            sums[h] = w if t == 0 else sums[h] + w
            o = jnp.dot(
                w.astype(jnp.bfloat16),
                tiles[t][TILE:, cols[h]],
                preferred_element_type=jnp.float32,
            )
            mixed[h] = o if t == 0 else mixed[h] + o
    total = {h: jnp.sum(sums[h], axis=1, keepdims=True) for h in heads}
    lane = lax.broadcasted_iota(jnp.int32, (TILE, HD), 1)
    stats = jnp.zeros((TILE, HD), jnp.float32)
    for h in heads:
        if normalise:
            any_live = top[h] > 0.5 * NONE
            total[h] = jnp.where(any_live, total[h], 0.0)
            mixed[h] = mixed[h] * jnp.where(any_live, 1.0 / total[h], 0.0)
        out[:, cols[h]] = mixed[h].astype(out.dtype)
        stats = jnp.where(lane == h, top[h], stats)
        stats = jnp.where(lane == STEP + h, total[h], stats)
    stats_out[...] = jnp.transpose(stats)[: 2 * STEP]


def attend(at, height_step, live, query, slots, normalise, name):
    tiles = [tile for slot, _ in slots_of(at) for tile in slots[slot]]
    pairs = len(tiles) * HEADS
    return pl.pallas_call(
        functools.partial(attend_kernel, at, height_step, len(tiles) // 3, normalise),
        out_shape=(
            jax.ShapeDtypeStruct((TILE, HEADS * HD), jnp.bfloat16 if normalise else jnp.float32),
            jax.ShapeDtypeStruct((2 * HEADS, HD), jnp.float32),
        ),
        grid=(HEADS // STEP,),
        in_specs=[IN_SMEM]
        + [pl.BlockSpec((2 * TILE, COL), lambda j: (0, j))] * (1 + len(tiles)),
        out_specs=(
            pl.BlockSpec((TILE, COL), lambda j: (0, j)),
            pl.BlockSpec((2 * STEP, HD), lambda j: (j, 0)),
        ),
        compiler_params=pltpu.CompilerParams(vmem_limit_bytes=VMEM),
        cost_estimate=pl.CostEstimate(
            flops=4 * pairs * TILE * TILE * HD,
            bytes_accessed=(len(tiles) + 2) * 2 * TILE * HEADS * HD * 2,
            transcendentals=pairs * TILE * TILE,
        ),
        name=name,
    )(live, query, *tiles)


def split_stats(stats):
    tops, totals = [], []
    for step in range(HEADS // STEP):
        start = step * 2 * STEP
        tops.append(stats[start : start + STEP])
        totals.append(stats[start + STEP : start + 2 * STEP])
    return jnp.concatenate(tops, axis=0), jnp.concatenate(totals, axis=0)


def combine_kernel(at, n_more, *refs):
    out, made, sem = refs[-3:]
    top, total = split_stats(refs[1][...])
    more = []
    best = top
    for m in range(n_more):
        top2, total2 = split_stats(refs[3 + 2 * m][...])
        top2 = jnp.where(total2 > 0.0, top2, NONE)
        more.append((top2, total2))
        best = jnp.maximum(best, top2)
    own = jnp.exp2((top - best) * C2)
    weights = [own]
    whole = total * own
    for top2, total2 in more:
        w = jnp.exp2((top2 - best) * C2) * total2
        weights.append(w)
        whole = whole + w
    inverse = 1.0 / whole
    weights = [w * inverse for w in weights]
    fill = TILE - HEADS * len(weights)
    columns = jnp.transpose(
        jnp.concatenate(weights + [jnp.zeros((fill, HD), jnp.float32)], axis=0)
    )
    for h in range(HEADS):
        cols = slice(h * HD, (h + 1) * HD)
        value = refs[0][:, cols] * columns[:, h : h + 1]
        for m in range(n_more):
            c = (m + 1) * HEADS + h
            value = value + refs[2 + 2 * m][:, cols].astype(jnp.float32) * columns[:, c : c + 1]
        made[:, cols] = value.astype(made.dtype)
    copy = pltpu.make_async_copy(made, out.at[rows_of(at)], sem)
    copy.start()
    copy.wait()


def combine(at, parts, n_more, into=None):
    specs = [IN_VMEM] * len(parts)
    extra, aliases = [], {}
    if into is not None:
        specs.append(ANYWHERE)
        extra, aliases = [into], {len(parts): 0}
    return pl.pallas_call(
        functools.partial(combine_kernel, at, n_more),
        out_shape=jax.ShapeDtypeStruct((2 * TILE, HEADS * HD), jnp.bfloat16),
        in_specs=specs,
        out_specs=ANYWHERE,
        scratch_shapes=[
            pltpu.VMEM((TILE, HEADS * HD), jnp.bfloat16),
            pltpu.SemaphoreType.DMA,
        ],
        input_output_aliases=aliases,
        compiler_params=pltpu.CompilerParams(vmem_limit_bytes=VMEM),
        name="combine",
    )(*parts, *extra)


def local(query, key, value, live):
    n_uly, n_blk = lax.axis_size("uly"), lax.axis_size("blk")
    high = n_blk // TW

    def blk_move(block, pairs):
        return lax.ppermute(block, "blk", pairs)

    def uly_shift(block, distance):
        pairs = [(i, i + distance) for i in range(n_uly) if 0 <= i + distance < n_uly]
        return lax.ppermute(block, "uly", pairs)

    def uly_swap(block):
        return lax.ppermute(block, "uly", [(0, 1), (1, 0)])

    def halo(first, second):
        if n_uly == 2:
            return [uly_swap(first)]
        return [uly_shift(second, 1), uly_shift(first, -1)]

    mate_pairs = [(i, i ^ 1) for i in range(n_blk)]
    outer_pairs = [(i, i - 1) for i in range(0, n_blk, 2) if i % TW > 0]
    outer_pairs += [(i, i + 1) for i in range(1, n_blk, 2) if i % TW < TW - 1]

    if high == 2:
        swap = [(i, (i + TW) % n_blk) for i in range(n_blk)]
        beside = [(swap, swap, None)]
    else:
        down = [(i, i + TW) for i in range(n_blk - TW)]
        up = [(i + TW, i) for i in range(n_blk - TW)]
        beside = [(down, up, 1), (up, down, -1)]

    far_queries = [blk_move(query, there) for there, _, _ in beside]
    first, second = pack(key, value)
    other_first = blk_move(first, outer_pairs)
    own_halo = halo(first, second)
    other_second = blk_move(second, outer_pairs)
    mate_first, mate_second = blk_move(first, mate_pairs), blk_move(second, mate_pairs)

    if n_uly == 2:
        other_live = uly_swap(live)
        other_first, other_live = lax.optimization_barrier((other_first, other_live))
        own_live = jnp.concatenate([live, other_live], axis=0).reshape(-1)
    else:
        own_live = lax.all_to_all(live, "uly", split_axis=1, concat_axis=0, tiled=True).reshape(-1)
    far_live = [blk_move(own_live, there) for there, _, _ in beside]
    other_halo = halo(other_first, other_second)

    def attend_beside(at, slots):
        return [
            list(attend(at, height_step, masks, queries, slots, True, "attend_beside"))
            for queries, masks, (_, _, height_step) in zip(far_queries, far_live, beside)
        ]

    slots = [(first, mate_first, other_first), (second, mate_second, other_second)]
    made = [None, None]
    if n_uly == 2:
        made[1] = attend_beside(1, slots)
        own_halo, other_halo, stats = lax.optimization_barrier(
            (own_halo, other_halo, [stats for _, stats in made[1]])
        )
        made[1] = [(part, late) for (part, _), late in zip(made[1], stats)]
    mate_halo = [blk_move(block, mate_pairs) for block in own_halo]
    slots += list(zip(own_halo, mate_halo, other_halo))
    for at in (1, 0):
        if made[at] is None:
            made[at] = attend_beside(at, slots)
    returned = [
        [blk_move(array, back) for pair, (_, back, _) in zip(made[at], beside) for array in pair]
        for at in range(2)
    ]
    own = [list(attend(at, 0, own_live, query, slots, False, "attend_own")) for at in range(2)]
    own, returned[1] = lax.optimization_barrier((own, returned[1]))
    out = None
    for at in (1, 0):
        out = combine(at, own[at] + returned[at], len(beside), out)
    return out


def solution(mesh):
    return jax.shard_map(
        local,
        mesh=mesh,
        in_specs=(
            P(("uly", "blk"), None),
            P(("uly", "blk"), None),
            P(("uly", "blk"), None),
            P("uly", None, "blk", None),
        ),
        out_specs=P(("uly", "blk"), None),
        check_vma=False,
    )
```

```python
import functools

import jax
import jax.numpy as jnp
from jax import lax
from jax.experimental import pallas as pl
from jax.experimental.pallas import tpu as pltpu
from jax.sharding import PartitionSpec as P

HD = 128
HEADS = 8
TILE = 128
TW = 8
NEAR = 27
STEP = 4
COL = STEP * HD
C2 = HD ** (-0.5) * 1.4426950408889634
NONE = -1e30
STAT_ROWS = 8
TERMS = 3
VMEM = 20 * 2**20

ANYWHERE = pl.BlockSpec(memory_space=pl.ANY)
IN_SMEM = pl.BlockSpec(memory_space=pltpu.SMEM)
IN_VMEM = pl.BlockSpec(memory_space=pltpu.VMEM)


def is_small():
    return lax.axis_size("uly") == 2 and lax.axis_size("blk") == 2 * TW


def frame_of(at):
    if is_small():
        g = lax.axis_index("uly")
        return 1 - g if at == 0 else g
    return at


def slots_of(at):
    if is_small():
        outward = 1 - 2 * lax.axis_index("uly")
        return ((0, 0), (1, -outward), (2, outward)) if at == 0 else ((0, outward), (1, 0))
    return ((0, 0), (1, 1), (2, -1)) if at == 0 else ((0, -1), (1, 0), (3, 1))


def rows_of(at):
    return pl.ds(pl.multiple_of(frame_of(at) * TILE, TILE), TILE)


def pack_kernel(key, value, both, border, sems):
    moves = []
    for row, (at, source) in enumerate(((1, key), (0, key), (0, value), (1, value))):
        moves.append((source.at[rows_of(at)], both.at[pl.ds(row * TILE, TILE)]))
    for half, source in enumerate((key, value)):
        moves.append((source.at[rows_of(0)], border.at[pl.ds(half * TILE, TILE)]))
    copies = [pltpu.make_async_copy(*move, sems.at[i]) for i, move in enumerate(moves)]
    for copy in copies:
        copy.start()
    for copy in copies:
        copy.wait()


def pack(key, value):
    def rows(tiles):
        return jax.ShapeDtypeStruct((tiles * TILE, HEADS * HD), key.dtype)

    return pl.pallas_call(
        pack_kernel,
        out_shape=(rows(4), rows(2)),
        in_specs=[ANYWHERE] * 2,
        out_specs=(IN_VMEM,) * 2,
        scratch_shapes=[pltpu.SemaphoreType.DMA((6,))],
        compiler_params=pltpu.CompilerParams(vmem_limit_bytes=VMEM),
        cost_estimate=pl.CostEstimate(flops=0, bytes_accessed=2**21, transcendentals=0),
        name="pack_kv",
    )(key, value)


def attend_kernel(at, which, height_step, places, travels, n_live, *refs):
    live, query, refs = refs[:n_live], refs[n_live], refs[n_live + 1 :]
    out, stats_out = (refs[-1], None) if travels else refs[-2:]
    step = pl.program_id(0)
    g, s = lax.axis_index("uly"), lax.axis_index("blk")
    height = 2 * (s // TW) - 1 if height_step is None else height_step
    width = 1 - 2 * (s % 2)
    offsets = {
        (slot, c): 9 * (frame_step + 1) + 3 * (height + 1) + width_step + 1
        for slot, frame_step in slots_of(at)
        for c, width_step in enumerate((0, width, -width))
    }

    def is_live(h, offset):
        head = step * STEP + h
        if is_small():
            held = HEADS // 2
            place = (which * held + lax.rem(head, held), 2 * g + frame_of(at), 0, offset)
            own_head = lax.div(head, held) == g
            return jnp.where(own_head, live[0][place], live[1][place]) > 0
        return live[0][head, frame_of(at), 0, offset] > 0

    heads = range(STEP)
    cols = [slice(h * HD, (h + 1) * HD) for h in heads]
    scores, highest = {}, {}
    for h in heads:
        q = query[rows_of(at), cols[h]]
        for block, (k_row, _, tiles) in enumerate(places):
            keys = refs[block][k_row : k_row + len(tiles) * TILE, cols[h]]
            score = lax.dot_general(
                q, keys, (((1,), (1,)), ((), ())), preferred_element_type=jnp.float32
            )
            for i, t in enumerate(tiles):
                part = score[:, i * TILE : (i + 1) * TILE]
                part = part + jnp.where(is_live(h, offsets[t]), 0.0, NONE)
                scores[h, t] = part
                highest[h] = jnp.maximum(highest[h], part) if h in highest else part
    top = {h: jnp.max(highest[h], axis=1, keepdims=True) for h in heads}
    shift = {h: top[h] * C2 for h in heads}
    mixed, sums = {}, {}
    for h in heads:
        for block, (_, v_row, tiles) in enumerate(places):
            weights = []
            for t in reversed(tiles):
                w = jnp.exp2(scores[h, t] * C2 - shift[h])
                sums[h] = sums[h] + w if h in sums else w
                weights.append(w.astype(jnp.bfloat16))
            values = refs[block][v_row : v_row + len(tiles) * TILE, cols[h]]
            o = jnp.dot(
                weights[0] if len(weights) == 1 else jnp.concatenate(weights, axis=1),
                values,
                preferred_element_type=jnp.float32,
            )
            mixed[h] = mixed[h] + o if h in mixed else o
    total = {h: jnp.sum(sums[h], axis=1, keepdims=True) for h in heads}
    lane = lax.broadcasted_iota(jnp.int32, (TILE, HD), 1)
    stats = jnp.zeros((TILE, HD), jnp.float32)
    for h in heads:
        if travels:
            any_live = top[h] > 0.5 * NONE
            total[h] = jnp.where(any_live, total[h], 0.0)
            mixed[h] = mixed[h] * jnp.where(any_live, 1.0 / total[h], 0.0)
        out[:TILE, cols[h]] = mixed[h].astype(out.dtype)
        stats = jnp.where(lane == h, top[h], stats)
        stats = jnp.where(lane == STEP + h, total[h], stats)
    stats = jnp.transpose(stats)[:STAT_ROWS]
    if travels:
        for term in range(TERMS):
            rounded = stats.astype(jnp.bfloat16)
            out[TILE:, cols[term]] = rounded
            stats = stats - rounded.astype(jnp.float32)
        out[TILE:, cols[TERMS]] = jnp.zeros((STAT_ROWS, HD), jnp.bfloat16)
    else:
        stats_out[...] = stats


def attend(at, which, height_step, live, query, both, beyond, travels, name, after):
    blocks = list(both)
    places = [(0, 2 * TILE, ((1, c), (0, c))) for c in range(3)]
    for slot, _ in slots_of(at)[2:]:
        blocks += beyond[slot - 2]
        places += [(0, TILE, ((slot, c),)) for c in range(3)]
    pairs = sum(len(tiles) for _, _, tiles in places) * HEADS
    steps = HEADS // STEP
    if travels:
        out_shape = jax.ShapeDtypeStruct((TILE + STAT_ROWS, HEADS * HD), jnp.bfloat16)
        out_specs = pl.BlockSpec((TILE + STAT_ROWS, COL), lambda j: (0, j))
    else:
        out_shape = (
            jax.ShapeDtypeStruct((TILE, HEADS * HD), jnp.float32),
            jax.ShapeDtypeStruct((steps * STAT_ROWS, HD), jnp.float32),
        )
        out_specs = (
            pl.BlockSpec((TILE, COL), lambda j: (0, j)),
            pl.BlockSpec((STAT_ROWS, HD), lambda j: (j, 0)),
        )
    return pl.pallas_call(
        functools.partial(attend_kernel, at, which, height_step, places, travels, len(live)),
        out_shape=out_shape,
        grid=(steps,),
        in_specs=[IN_SMEM] * len(live)
        + [pl.BlockSpec((array.shape[0], COL), lambda j: (0, j)) for array in [query] + blocks]
        + [ANYWHERE] * len(after),
        out_specs=out_specs,
        compiler_params=pltpu.CompilerParams(vmem_limit_bytes=VMEM),
        cost_estimate=pl.CostEstimate(
            flops=4 * pairs * TILE * TILE * HD,
            bytes_accessed=(pairs // HEADS + 2) * 2 * TILE * HEADS * HD * 2,
            transcendentals=pairs * TILE * TILE,
        ),
        name=name,
    )(*live, query, *blocks, *after)


def split_stats(per_step):
    tops = jnp.concatenate([stats[:STEP] for stats in per_step], axis=0)
    totals = jnp.concatenate([stats[STEP : 2 * STEP] for stats in per_step], axis=0)
    return tops, totals


def own_stats(ref):
    steps = range(HEADS // STEP)
    return split_stats([ref[step * STAT_ROWS : (step + 1) * STAT_ROWS] for step in steps])


def travelled_stats(ref):
    per_step = []
    for step in range(HEADS // STEP):
        first = step * COL
        terms = [ref[TILE:, first + HD * t : first + HD * (t + 1)] for t in range(TERMS)]
        per_step.append(sum(term.astype(jnp.float32) for term in terms))
    return split_stats(per_step)


def combine_kernel(at, n_more, *refs):
    out, made, sem = refs[-3:]
    top, total = own_stats(refs[1])
    more = []
    best = top
    for m in range(n_more):
        top2, total2 = travelled_stats(refs[2 + m])
        top2 = jnp.where(total2 > 0.0, top2, NONE)
        more.append((top2, total2))
        best = jnp.maximum(best, top2)
    own = jnp.exp2((top - best) * C2)
    weights = [own]
    whole = total * own
    for top2, total2 in more:
        w = jnp.exp2((top2 - best) * C2) * total2
        weights.append(w)
        whole = whole + w
    inverse = 1.0 / whole
    weights = [w * inverse for w in weights]
    fill = TILE - HEADS * len(weights)
    columns = jnp.transpose(
        jnp.concatenate(weights + [jnp.zeros((fill, HD), jnp.float32)], axis=0)
    )
    for h in range(HEADS):
        cols = slice(h * HD, (h + 1) * HD)
        value = refs[0][:, cols] * columns[:, h : h + 1]
        for m in range(n_more):
            c = (m + 1) * HEADS + h
            value = value + refs[2 + m][:TILE, cols].astype(jnp.float32) * columns[:, c : c + 1]
        made[:, cols] = value.astype(made.dtype)
    copy = pltpu.make_async_copy(made, out.at[rows_of(at)], sem)
    copy.start()
    copy.wait()


def combine(at, parts, n_more, into=None):
    specs = [IN_VMEM] * len(parts)
    extra, aliases = [], {}
    if into is not None:
        specs.append(ANYWHERE)
        extra, aliases = [into], {len(parts): 0}
    return pl.pallas_call(
        functools.partial(combine_kernel, at, n_more),
        out_shape=jax.ShapeDtypeStruct((2 * TILE, HEADS * HD), jnp.bfloat16),
        in_specs=specs,
        out_specs=ANYWHERE,
        scratch_shapes=[
            pltpu.VMEM((TILE, HEADS * HD), jnp.bfloat16),
            pltpu.SemaphoreType.DMA,
        ],
        input_output_aliases=aliases,
        compiler_params=pltpu.CompilerParams(vmem_limit_bytes=VMEM),
        name="combine",
    )(*parts, *extra)


def local(query, key, value, live):
    n_uly, n_blk = lax.axis_size("uly"), lax.axis_size("blk")
    high = n_blk // TW

    def blk_move(block, pairs):
        return lax.ppermute(block, "blk", pairs)

    def uly_shift(block, distance):
        pairs = [(i, i + distance) for i in range(n_uly) if 0 <= i + distance < n_uly]
        return lax.ppermute(block, "uly", pairs)

    def uly_swap(block):
        return lax.ppermute(block, "uly", [(0, 1), (1, 0)])

    def halo(both, border):
        if is_small():
            return [uly_swap(border)]
        after = jnp.concatenate([both[:TILE], both[3 * TILE :]], axis=0)
        return [uly_shift(after, 1), uly_shift(border_of(both), -1)]

    def border_of(both):
        return both[TILE : 3 * TILE]

    mate_pairs = [(i, i ^ 1) for i in range(n_blk)]
    outer_pairs = [(i, i - 1) for i in range(0, n_blk, 2) if i % TW > 0]
    outer_pairs += [(i, i + 1) for i in range(1, n_blk, 2) if i % TW < TW - 1]

    if high == 2:
        swap = [(i, (i + TW) % n_blk) for i in range(n_blk)]
        beside = [(swap, swap, None)]
    else:
        down = [(i, i + TW) for i in range(n_blk - TW)]
        up = [(i + TW, i) for i in range(n_blk - TW)]
        beside = [(down, up, 1), (up, down, -1)]

    both, border = pack(key, value)
    if is_small():
        far_live = blk_move(live, beside[0][0])
        far_live, query, both = lax.optimization_barrier((far_live, query, both))
        held = ((0, len(live), 0), (0, 0, 0), (0, 0, 0), (0, 0, 0))
        below = ((len(live), 0, 0), (0, 0, 0), (0, 0, 0), (0, 0, 0))
        live = lax.pad(live, 0, held) + lax.pad(far_live, 0, below)
        other_live = uly_swap(live)
        border, other_live = lax.optimization_barrier((border, other_live))
        own_live, far_live = [live, other_live], [[live, other_live]]
    else:
        own_live = [lax.all_to_all(live, "uly", split_axis=1, concat_axis=0, tiled=True)]
        far_live = [[blk_move(own_live[0], there)] for there, _, _ in beside]
    far_queries = [blk_move(query, there) for there, _, _ in beside]
    other = blk_move(both, outer_pairs)
    mate = blk_move(both, mate_pairs)
    own_halo = halo(both, border)
    other_halo = halo(other, border_of(other))

    def attend_beside(at, after):
        return [
            attend(at, 1, height_step, masks, block, blocks, beyond, True, "attend_beside", after)
            for block, masks, (_, _, height_step) in zip(far_queries, far_live, beside)
        ]

    blocks, beyond = (both, mate, other), []
    made = [None, None]
    after = []
    if is_small():
        made[1] = attend_beside(1, [])
        own_halo, after = lax.optimization_barrier((own_halo, made[1]))
    mate_halo = [blk_move(block, mate_pairs) for block in own_halo]
    beyond += [list(halos) for halos in zip(own_halo, mate_halo, other_halo)]
    if not is_small():
        made[1] = attend_beside(1, [])
    made[0] = attend_beside(0, after)
    returned = [
        [blk_move(part, back) for part, (_, back, _) in zip(made[at], beside)] for at in range(2)
    ]
    own = [
        attend(at, 0, 0, own_live, query, blocks, beyond, False, "attend_own", [])
        for at in range(2)
    ]
    own, returned[1] = lax.optimization_barrier((own, returned[1]))
    out = None
    for at in (1, 0):
        out = combine(at, list(own[at]) + returned[at], len(beside), out)
    return out


def solution(mesh):
    return jax.shard_map(
        local,
        mesh=mesh,
        in_specs=(
            P(("uly", "blk"), None),
            P(("uly", "blk"), None),
            P(("uly", "blk"), None),
            P("uly", None, "blk", None),
        ),
        out_specs=P(("uly", "blk"), None),
        check_vma=False,
    )
```

```python
import functools

import jax
import jax.numpy as jnp
from jax import lax
from jax.experimental import pallas as pl
from jax.experimental.pallas import tpu as pltpu
from jax.sharding import PartitionSpec as P

HD = 128
HEADS = 8
TILE = 128
TW = 8
NEAR = 27
STEP = 4
COL = STEP * HD
C2 = HD ** (-0.5) * 1.4426950408889634
NONE = -1e30
STAT_ROWS = 8
TERMS = 3
VMEM = 20 * 2**20

ANYWHERE = pl.BlockSpec(memory_space=pl.ANY)
IN_SMEM = pl.BlockSpec(memory_space=pltpu.SMEM)
IN_VMEM = pl.BlockSpec(memory_space=pltpu.VMEM)


def is_small():
    return lax.axis_size("uly") == 2 and lax.axis_size("blk") == 2 * TW


def frame_of(at):
    if is_small():
        g = lax.axis_index("uly")
        return 1 - g if at == 0 else g
    return at


def slots_of(at):
    if is_small():
        outward = 1 - 2 * lax.axis_index("uly")
        return ((0, 0), (1, -outward), (2, outward)) if at == 0 else ((0, outward), (1, 0))
    return ((0, 0), (1, 1), (2, -1)) if at == 0 else ((0, -1), (1, 0), (3, 1))


def rows_of(at):
    return pl.ds(pl.multiple_of(frame_of(at) * TILE, TILE), TILE)


def pack_kernel(key, value, both, border, inner, sems):
    loads = {}
    for row, (at, half, source) in enumerate(((1, 0, key), (0, 0, key), (0, 1, value), (1, 1, value))):
        to = both.at[pl.ds(row * TILE, TILE)]
        loads[at, half] = pltpu.make_async_copy(source.at[rows_of(at)], to, sems.at[row])
    for at in range(2):
        for half in range(2):
            loads[at, half].start()
    for half in range(2):
        loads[0, half].wait()
    border[...] = both[TILE : 3 * TILE]
    for half in range(2):
        loads[1, half].wait()
    inner[:TILE] = both[:TILE]
    inner[TILE:] = both[3 * TILE :]


def pack(key, value):
    def rows(tiles):
        return jax.ShapeDtypeStruct((tiles * TILE, HEADS * HD), key.dtype)

    return pl.pallas_call(
        pack_kernel,
        out_shape=(rows(4), rows(2), rows(2)),
        in_specs=[pl.BlockSpec(memory_space=pltpu.HBM)] * 2,
        out_specs=(IN_VMEM,) * 3,
        scratch_shapes=[pltpu.SemaphoreType.DMA((4,))],
        compiler_params=pltpu.CompilerParams(vmem_limit_bytes=VMEM),
        cost_estimate=pl.CostEstimate(flops=0, bytes_accessed=2**21, transcendentals=0),
        name="pack_kv",
    )(key, value)


def attend_kernel(at, which, height_step, places, travels, n_live, *refs):
    live, query, refs = refs[:n_live], refs[n_live], refs[n_live + 1 :]
    out, stats_out = (refs[-1], None) if travels else refs[-2:]
    g, s = lax.axis_index("uly"), lax.axis_index("blk")
    height = 2 * (s // TW) - 1 if height_step is None else height_step
    width = 1 - 2 * (s % 2)
    offsets = {
        (slot, c): 9 * (frame_step + 1) + 3 * (height + 1) + width_step + 1
        for slot, frame_step in slots_of(at)
        for c, width_step in enumerate((0, width, -width))
    }
    rows = rows_of(at)
    lane = lax.broadcasted_iota(jnp.int32, (TILE, HD), 1)

    def is_live(head, offset):
        if is_small():
            held = HEADS // 2
            place = (which * held + head % held, 2 * g + frame_of(at), 0, offset)
            return jnp.where(g == head // held, live[0][place], live[1][place]) > 0
        return live[0][head, frame_of(at), 0, offset] > 0

    cols = [slice(h * HD, (h + 1) * HD) for h in range(HEADS)]
    for step in range(HEADS // STEP):
        heads = range(step * STEP, (step + 1) * STEP)
        scores, highest = {}, {}
        for h in heads:
            q = query[rows, cols[h]]
            for block, (k_row, _, tiles) in enumerate(places):
                keys = refs[block][k_row : k_row + len(tiles) * TILE, cols[h]]
                score = lax.dot_general(
                    q, keys, (((1,), (1,)), ((), ())), preferred_element_type=jnp.float32
                )
                for i, t in enumerate(tiles):
                    part = score[:, i * TILE : (i + 1) * TILE]
                    part = part + jnp.where(is_live(h, offsets[t]), 0.0, NONE)
                    scores[h, t] = part
                    highest[h] = jnp.maximum(highest[h], part) if h in highest else part
        top = {h: jnp.max(highest[h], axis=1, keepdims=True) for h in heads}
        shift = {h: top[h] * C2 for h in heads}
        mixed, sums = {}, {}
        for h in heads:
            for block, (_, v_row, tiles) in enumerate(places):
                weights = []
                for t in reversed(tiles):
                    w = jnp.exp2(scores[h, t] * C2 - shift[h])
                    sums[h] = sums[h] + w if h in sums else w
                    weights.append(w.astype(jnp.bfloat16))
                values = refs[block][v_row : v_row + len(tiles) * TILE, cols[h]]
                o = jnp.dot(
                    weights[0] if len(weights) == 1 else jnp.concatenate(weights, axis=1),
                    values,
                    preferred_element_type=jnp.float32,
                )
                mixed[h] = mixed[h] + o if h in mixed else o
        total = {h: jnp.sum(sums[h], axis=1, keepdims=True) for h in heads}
        stats = jnp.zeros((TILE, HD), jnp.float32)
        for i, h in enumerate(heads):
            if travels:
                any_live = top[h] > 0.5 * NONE
                total[h] = jnp.where(any_live, total[h], 0.0)
                mixed[h] = mixed[h] * jnp.where(any_live, 1.0 / total[h], 0.0)
            out[:TILE, cols[h]] = mixed[h].astype(out.dtype)
            stats = jnp.where(lane == i, top[h], stats)
            stats = jnp.where(lane == STEP + i, total[h], stats)
        stats = jnp.transpose(stats)[:STAT_ROWS]
        if travels:
            for term in range(TERMS):
                rounded = stats.astype(jnp.bfloat16)
                out[TILE:, cols[heads[term]]] = rounded
                stats = stats - rounded.astype(jnp.float32)
            out[TILE:, cols[heads[TERMS]]] = jnp.zeros((STAT_ROWS, HD), jnp.bfloat16)
        else:
            stats_out[step * STAT_ROWS : (step + 1) * STAT_ROWS] = stats


def attend(at, which, height_step, live, query, both, beyond, travels, name, after):
    blocks = list(both)
    places = [(0, 2 * TILE, ((1, c), (0, c))) for c in range(2)]
    places += [(0, TILE, ((slot, 2),)) for slot in range(2)]
    for slot, _ in slots_of(at)[2:]:
        blocks += beyond[slot - 2]
        places += [(0, TILE, ((slot, c),)) for c in range(3)]
    pairs = sum(len(tiles) for _, _, tiles in places) * HEADS
    steps = HEADS // STEP
    if travels:
        out_shape = jax.ShapeDtypeStruct((TILE + STAT_ROWS, HEADS * HD), jnp.bfloat16)
    else:
        out_shape = (
            jax.ShapeDtypeStruct((TILE, HEADS * HD), jnp.float32),
            jax.ShapeDtypeStruct((steps * STAT_ROWS, HD), jnp.float32),
        )
    return pl.pallas_call(
        functools.partial(attend_kernel, at, which, height_step, places, travels, len(live)),
        out_shape=out_shape,
        in_specs=[IN_SMEM] * len(live) + [IN_VMEM] * (1 + len(blocks)) + [ANYWHERE] * len(after),
        out_specs=IN_VMEM if travels else (IN_VMEM, IN_VMEM),
        compiler_params=pltpu.CompilerParams(vmem_limit_bytes=VMEM),
        cost_estimate=pl.CostEstimate(
            flops=4 * pairs * TILE * TILE * HD,
            bytes_accessed=(pairs // HEADS + 2) * 2 * TILE * HEADS * HD * 2,
            transcendentals=pairs * TILE * TILE,
        ),
        name=name,
    )(*live, query, *blocks, *after)


def split_stats(per_step):
    tops = jnp.concatenate([stats[:STEP] for stats in per_step], axis=0)
    totals = jnp.concatenate([stats[STEP : 2 * STEP] for stats in per_step], axis=0)
    return tops, totals


def own_stats(ref):
    steps = range(HEADS // STEP)
    return split_stats([ref[step * STAT_ROWS : (step + 1) * STAT_ROWS] for step in steps])


def travelled_stats(ref):
    per_step = []
    for step in range(HEADS // STEP):
        first = step * COL
        terms = [ref[TILE:, first + HD * t : first + HD * (t + 1)] for t in range(TERMS)]
        per_step.append(sum(term.astype(jnp.float32) for term in terms))
    return split_stats(per_step)


def combine_kernel(at, n_more, *refs):
    out, made, sem = refs[-3:]
    travelled, (mine, stats) = refs[:n_more], refs[n_more : n_more + 2]
    top, total = own_stats(stats)
    more = []
    best = top
    for m in range(n_more):
        top2, total2 = travelled_stats(travelled[m])
        top2 = jnp.where(total2 > 0.0, top2, NONE)
        more.append((top2, total2))
        best = jnp.maximum(best, top2)
    own = jnp.exp2((top - best) * C2)
    weights = [own]
    whole = total * own
    for top2, total2 in more:
        w = jnp.exp2((top2 - best) * C2) * total2
        weights.append(w)
        whole = whole + w
    inverse = 1.0 / whole
    weights = [w * inverse for w in weights]
    fill = TILE - HEADS * len(weights)
    columns = jnp.transpose(
        jnp.concatenate(weights + [jnp.zeros((fill, HD), jnp.float32)], axis=0)
    )
    for h in range(HEADS):
        cols = slice(h * HD, (h + 1) * HD)
        value = mine[:, cols] * columns[:, h : h + 1]
        for m in range(n_more):
            c = (m + 1) * HEADS + h
            value = value + travelled[m][:TILE, cols].astype(jnp.float32) * columns[:, c : c + 1]
        made[:, cols] = value.astype(made.dtype)
    copy = pltpu.make_async_copy(made, out.at[rows_of(at)], sem)
    copy.start()
    copy.wait()


def combine(at, parts, n_more, into=None):
    specs = [IN_VMEM] * len(parts)
    extra, aliases = [], {}
    if into is not None:
        specs.append(ANYWHERE)
        extra, aliases = [into], {len(parts): 0}
    return pl.pallas_call(
        functools.partial(combine_kernel, at, n_more),
        out_shape=jax.ShapeDtypeStruct((2 * TILE, HEADS * HD), jnp.bfloat16),
        in_specs=specs,
        out_specs=ANYWHERE,
        scratch_shapes=[
            pltpu.VMEM((TILE, HEADS * HD), jnp.bfloat16),
            pltpu.SemaphoreType.DMA,
        ],
        input_output_aliases=aliases,
        compiler_params=pltpu.CompilerParams(vmem_limit_bytes=VMEM),
        name="combine",
    )(*parts, *extra)


def local(query, key, value, live):
    n_uly, n_blk = lax.axis_size("uly"), lax.axis_size("blk")
    high = n_blk // TW

    def blk_move(block, pairs):
        return lax.ppermute(block, "blk", pairs)

    def uly_shift(block, distance):
        pairs = [(i, i + distance) for i in range(n_uly) if 0 <= i + distance < n_uly]
        return lax.ppermute(block, "uly", pairs)

    def uly_swap(block):
        return lax.ppermute(block, "uly", [(0, 1), (1, 0)])

    def halo(first, second):
        if is_small():
            return [uly_swap(first)]
        return [uly_shift(second, 1), uly_shift(first, -1)]

    mate_pairs = [(i, i ^ 1) for i in range(n_blk)]
    outer_pairs = [(i, i - 1) for i in range(0, n_blk, 2) if i % TW > 0]
    outer_pairs += [(i, i + 1) for i in range(1, n_blk, 2) if i % TW < TW - 1]

    if high == 2:
        swap = [(i, (i + TW) % n_blk) for i in range(n_blk)]
        beside = [(swap, swap, None)]
    else:
        down = [(i, i + TW) for i in range(n_blk - TW)]
        up = [(i + TW, i) for i in range(n_blk - TW)]
        beside = [(down, up, 1), (up, down, -1)]

    key, value = (pltpu.with_memory_space_constraint(a, pltpu.HBM) for a in (key, value))
    both, border, inner = pack(key, value)
    if is_small():
        far_live = blk_move(live, beside[0][0])
        far_live, query, both, border, inner = lax.optimization_barrier(
            (far_live, query, both, border, inner)
        )
        held = ((0, len(live), 0), (0, 0, 0), (0, 0, 0), (0, 0, 0))
        below = ((len(live), 0, 0), (0, 0, 0), (0, 0, 0), (0, 0, 0))
        live = lax.pad(live, 0, held) + lax.pad(far_live, 0, below)
        other_live = uly_swap(live)
        other_first = border
        border, other_live = lax.optimization_barrier((border, other_live))
        own_live, far_live = [live, other_live], [[live, other_live]]
    else:
        other_first = border
        own_live = [lax.all_to_all(live, "uly", split_axis=1, concat_axis=0, tiled=True)]
        far_live = [[blk_move(own_live[0], there)] for there, _, _ in beside]
    far_queries = [blk_move(query, there) for there, _, _ in beside]
    other_border = blk_move(other_first, outer_pairs)
    other_inner = blk_move(inner, outer_pairs)
    mate = blk_move(both, mate_pairs)
    own_halo = halo(border, inner)
    if is_small():
        token = blk_move(other_border[:TILE], mate_pairs)
        other_border, token = lax.optimization_barrier((other_border, token))
    other_halo = halo(other_border, other_inner)

    def attend_beside(at, after):
        return [
            attend(at, 1, height_step, masks, block, blocks, beyond, True, "attend_beside", after)
            for block, masks, (_, _, height_step) in zip(far_queries, far_live, beside)
        ]

    blocks, beyond = (both, mate, other_border, other_inner), []
    made = [None, None]
    after = []
    if is_small():
        made[1] = attend_beside(1, [])
        own_halo, after = lax.optimization_barrier((own_halo, made[1]))
        after = after + [token]
    mate_halo = [blk_move(block, mate_pairs) for block in own_halo]
    beyond += [list(halos) for halos in zip(own_halo, mate_halo, other_halo)]
    if not is_small():
        made[1] = attend_beside(1, [])
    made[0] = attend_beside(0, after)
    returned = [
        [blk_move(part, back) for part, (_, back, _) in zip(made[at], beside)] for at in range(2)
    ]
    own = [
        attend(at, 0, 0, own_live, query, blocks, beyond, False, "attend_own", [])
        for at in range(2)
    ]
    returned[1], own = lax.optimization_barrier((returned[1], own))
    out = None
    for at in (1, 0):
        out = combine(at, returned[at] + list(own[at]), len(beside), out)
    return out


def solution(mesh):
    return jax.shard_map(
        local,
        mesh=mesh,
        in_specs=(
            P(("uly", "blk"), None),
            P(("uly", "blk"), None),
            P(("uly", "blk"), None),
            P("uly", None, "blk", None),
        ),
        out_specs=P(("uly", "blk"), None),
        check_vma=False,
    )
```

```python
import functools

import jax
import jax.numpy as jnp
from jax import lax
from jax.experimental import pallas as pl
from jax.experimental.pallas import tpu as pltpu
from jax.sharding import PartitionSpec as P

HD = 128
HEADS = 8
TILE = 128
TW = 8
NEAR = 27
STEP = 4
COL = STEP * HD
C2 = HD ** (-0.5) * 1.4426950408889634
NONE = -1e30
STAT_ROWS = 8
TERMS = 3
VMEM = 20 * 2**20

ANYWHERE = pl.BlockSpec(memory_space=pl.ANY)
IN_SMEM = pl.BlockSpec(memory_space=pltpu.SMEM)
IN_VMEM = pl.BlockSpec(memory_space=pltpu.VMEM)


def is_small():
    return lax.axis_size("uly") == 2 and lax.axis_size("blk") == 2 * TW


def frame_of(at):
    if is_small():
        g = lax.axis_index("uly")
        return 1 - g if at == 0 else g
    return at


def slots_of(at):
    if is_small():
        outward = 1 - 2 * lax.axis_index("uly")
        return ((0, 0), (1, -outward), (2, outward)) if at == 0 else ((0, outward), (1, 0))
    return ((0, 0), (1, 1), (2, -1)) if at == 0 else ((0, -1), (1, 0), (3, 1))


def rows_of(at):
    return pl.ds(pl.multiple_of(frame_of(at) * TILE, TILE), TILE)


def pack_kernel(key, value, both, border, inner, sems):
    loads = {}
    for row, (at, half, source) in enumerate(((1, 0, key), (0, 0, key), (0, 1, value), (1, 1, value))):
        to = both.at[pl.ds(row * TILE, TILE)]
        loads[at, half] = pltpu.make_async_copy(source.at[rows_of(at)], to, sems.at[row])
    for at in range(2):
        for half in range(2):
            loads[at, half].start()
    for half in range(2):
        loads[0, half].wait()
    border[...] = both[TILE : 3 * TILE]
    for half in range(2):
        loads[1, half].wait()
    inner[:TILE] = both[:TILE]
    inner[TILE:] = both[3 * TILE :]


def pack(key, value):
    def rows(tiles):
        return jax.ShapeDtypeStruct((tiles * TILE, HEADS * HD), key.dtype)

    return pl.pallas_call(
        pack_kernel,
        out_shape=(rows(4), rows(2), rows(2)),
        in_specs=[pl.BlockSpec(memory_space=pltpu.HBM)] * 2,
        out_specs=(IN_VMEM,) * 3,
        scratch_shapes=[pltpu.SemaphoreType.DMA((4,))],
        compiler_params=pltpu.CompilerParams(vmem_limit_bytes=VMEM),
        cost_estimate=pl.CostEstimate(flops=0, bytes_accessed=2**21, transcendentals=0),
        name="pack_kv",
    )(key, value)


def bias_kernel(which, height_step, n_live, *refs):
    live, out = refs[:n_live], refs[n_live]
    g, s = lax.axis_index("uly"), lax.axis_index("blk")
    height = 2 * (s // TW) - 1 if height_step is None else height_step
    width = 1 - 2 * (s % 2)

    def is_live(at, head, offset):
        if is_small():
            held = HEADS // 2
            place = (which * held + head % held, 2 * g + frame_of(at), 0, offset)
            return jnp.where(g == head // held, live[0][place], live[1][place]) > 0
        return live[0][head, frame_of(at), 0, offset] > 0

    for at in range(2):
        for slot, frame_step in slots_of(at):
            for c, width_step in enumerate((0, width, -width)):
                offset = 9 * (frame_step + 1) + 3 * (height + 1) + width_step + 1
                for head in range(HEADS):
                    row = bias_row(at, slot, c, head)
                    bias = jnp.where(is_live(at, head, offset), 0.0, NONE)
                    out[row : row + 1] = jnp.full((1, HD), bias, jnp.float32)


def bias_row(at, slot, c, head):
    counts = [len(slots_of(part)) for part in range(2)]
    order = [number for number, _ in slots_of(at)].index(slot)
    return ((counts[0] * HEADS if at else 0) + head * counts[at] + order) * 3 + c


def biases(which, height_step, live, name):
    rows = sum(len(slots_of(at)) for at in range(2)) * HEADS * 3
    return pl.pallas_call(
        functools.partial(bias_kernel, which, height_step, len(live)),
        out_shape=jax.ShapeDtypeStruct((rows, HD), jnp.float32),
        in_specs=[IN_SMEM] * len(live),
        out_specs=IN_VMEM,
        compiler_params=pltpu.CompilerParams(vmem_limit_bytes=VMEM),
        name=name,
    )(*live)


def attend_kernel(at, places, travels, bias, query, *refs):
    out, stats_out = (refs[-1], None) if travels else refs[-2:]
    rows = rows_of(at)
    lane = lax.broadcasted_iota(jnp.int32, (TILE, HD), 1)

    cols = [slice(h * HD, (h + 1) * HD) for h in range(HEADS)]
    for step in range(HEADS // STEP):
        heads = range(step * STEP, (step + 1) * STEP)
        scores, highest = {}, {}
        for h in heads:
            q = query[rows, cols[h]]
            for block, (k_row, _, tiles) in enumerate(places):
                keys = refs[block][k_row : k_row + len(tiles) * TILE, cols[h]]
                score = lax.dot_general(
                    q, keys, (((1,), (1,)), ((), ())), preferred_element_type=jnp.float32
                )
                for i, t in enumerate(tiles):
                    part = score[:, i * TILE : (i + 1) * TILE]
                    row = bias_row(at, *t, h)
                    part = part + bias[row : row + 1]
                    scores[h, t] = part
                    highest[h] = jnp.maximum(highest[h], part) if h in highest else part
        top = {h: jnp.max(highest[h], axis=1, keepdims=True) for h in heads}
        shift = {h: top[h] * C2 for h in heads}
        mixed, sums = {}, {}
        for h in heads:
            for block, (_, v_row, tiles) in enumerate(places):
                weights = []
                for t in reversed(tiles):
                    w = jnp.exp2(scores[h, t] * C2 - shift[h])
                    sums[h] = sums[h] + w if h in sums else w
                    weights.append(w.astype(jnp.bfloat16))
                values = refs[block][v_row : v_row + len(tiles) * TILE, cols[h]]
                o = jnp.dot(
                    weights[0] if len(weights) == 1 else jnp.concatenate(weights, axis=1),
                    values,
                    preferred_element_type=jnp.float32,
                )
                mixed[h] = mixed[h] + o if h in mixed else o
        total = {h: jnp.sum(sums[h], axis=1, keepdims=True) for h in heads}
        stats = jnp.zeros((TILE, HD), jnp.float32)
        for i, h in enumerate(heads):
            if travels:
                any_live = top[h] > 0.5 * NONE
                total[h] = jnp.where(any_live, total[h], 0.0)
                mixed[h] = mixed[h] * jnp.where(any_live, 1.0 / total[h], 0.0)
            out[:TILE, cols[h]] = mixed[h].astype(out.dtype)
            stats = jnp.where(lane == i, top[h], stats)
            stats = jnp.where(lane == STEP + i, total[h], stats)
        stats = jnp.transpose(stats)[:STAT_ROWS]
        if travels:
            for term in range(TERMS):
                rounded = stats.astype(jnp.bfloat16)
                out[TILE:, cols[heads[term]]] = rounded
                stats = stats - rounded.astype(jnp.float32)
            out[TILE:, cols[heads[TERMS]]] = jnp.zeros((STAT_ROWS, HD), jnp.bfloat16)
        else:
            stats_out[step * STAT_ROWS : (step + 1) * STAT_ROWS] = stats


def attend(at, bias, query, both, beyond, travels, name, after):
    blocks = list(both)
    places = [(0, 2 * TILE, ((1, c), (0, c))) for c in range(2)]
    places += [(0, TILE, ((slot, 2),)) for slot in range(2)]
    for slot, _ in slots_of(at)[2:]:
        blocks += beyond[slot - 2]
        places += [(0, TILE, ((slot, c),)) for c in range(3)]
    pairs = sum(len(tiles) for _, _, tiles in places) * HEADS
    steps = HEADS // STEP
    if travels:
        out_shape = jax.ShapeDtypeStruct((TILE + STAT_ROWS, HEADS * HD), jnp.bfloat16)
    else:
        out_shape = (
            jax.ShapeDtypeStruct((TILE, HEADS * HD), jnp.float32),
            jax.ShapeDtypeStruct((steps * STAT_ROWS, HD), jnp.float32),
        )
    return pl.pallas_call(
        functools.partial(attend_kernel, at, places, travels),
        out_shape=out_shape,
        in_specs=[IN_VMEM] * (2 + len(blocks)) + [ANYWHERE] * len(after),
        out_specs=IN_VMEM if travels else (IN_VMEM, IN_VMEM),
        compiler_params=pltpu.CompilerParams(vmem_limit_bytes=VMEM),
        cost_estimate=pl.CostEstimate(
            flops=4 * pairs * TILE * TILE * HD,
            bytes_accessed=(pairs // HEADS + 2) * 2 * TILE * HEADS * HD * 2,
            transcendentals=pairs * TILE * TILE,
        ),
        name=name,
    )(bias, query, *blocks, *after)


def split_stats(per_step):
    tops = jnp.concatenate([stats[:STEP] for stats in per_step], axis=0)
    totals = jnp.concatenate([stats[STEP : 2 * STEP] for stats in per_step], axis=0)
    return tops, totals


def own_stats(ref):
    steps = range(HEADS // STEP)
    return split_stats([ref[step * STAT_ROWS : (step + 1) * STAT_ROWS] for step in steps])


def travelled_stats(ref):
    per_step = []
    for step in range(HEADS // STEP):
        first = step * COL
        terms = [ref[TILE:, first + HD * t : first + HD * (t + 1)] for t in range(TERMS)]
        per_step.append(sum(term.astype(jnp.float32) for term in terms))
    return split_stats(per_step)


def combine_kernel(at, n_more, *refs):
    out, made, sem = refs[-3:]
    travelled, (mine, stats) = refs[:n_more], refs[n_more : n_more + 2]
    top, total = own_stats(stats)
    more = []
    best = top
    for m in range(n_more):
        top2, total2 = travelled_stats(travelled[m])
        top2 = jnp.where(total2 > 0.0, top2, NONE)
        more.append((top2, total2))
        best = jnp.maximum(best, top2)
    own = jnp.exp2((top - best) * C2)
    weights = [own]
    whole = total * own
    for top2, total2 in more:
        w = jnp.exp2((top2 - best) * C2) * total2
        weights.append(w)
        whole = whole + w
    inverse = 1.0 / whole
    weights = [w * inverse for w in weights]
    fill = TILE - HEADS * len(weights)
    columns = jnp.transpose(
        jnp.concatenate(weights + [jnp.zeros((fill, HD), jnp.float32)], axis=0)
    )
    for h in range(HEADS):
        cols = slice(h * HD, (h + 1) * HD)
        value = mine[:, cols] * columns[:, h : h + 1]
        for m in range(n_more):
            c = (m + 1) * HEADS + h
            value = value + travelled[m][:TILE, cols].astype(jnp.float32) * columns[:, c : c + 1]
        made[:, cols] = value.astype(made.dtype)
    copy = pltpu.make_async_copy(made, out.at[rows_of(at)], sem)
    copy.start()
    copy.wait()


def combine(at, parts, n_more, into=None):
    specs = [IN_VMEM] * len(parts)
    extra, aliases = [], {}
    if into is not None:
        specs.append(ANYWHERE)
        extra, aliases = [into], {len(parts): 0}
    return pl.pallas_call(
        functools.partial(combine_kernel, at, n_more),
        out_shape=jax.ShapeDtypeStruct((2 * TILE, HEADS * HD), jnp.bfloat16),
        in_specs=specs,
        out_specs=ANYWHERE,
        scratch_shapes=[
            pltpu.VMEM((TILE, HEADS * HD), jnp.bfloat16),
            pltpu.SemaphoreType.DMA,
        ],
        input_output_aliases=aliases,
        compiler_params=pltpu.CompilerParams(vmem_limit_bytes=VMEM),
        name="combine",
    )(*parts, *extra)


def local(query, key, value, live):
    n_uly, n_blk = lax.axis_size("uly"), lax.axis_size("blk")
    high = n_blk // TW

    def blk_move(block, pairs):
        return lax.ppermute(block, "blk", pairs)

    def uly_shift(block, distance):
        pairs = [(i, i + distance) for i in range(n_uly) if 0 <= i + distance < n_uly]
        return lax.ppermute(block, "uly", pairs)

    def uly_swap(block):
        return lax.ppermute(block, "uly", [(0, 1), (1, 0)])

    def halo(first, second):
        if is_small():
            return [uly_swap(first)]
        return [uly_shift(second, 1), uly_shift(first, -1)]

    mate_pairs = [(i, i ^ 1) for i in range(n_blk)]
    outer_pairs = [(i, i - 1) for i in range(0, n_blk, 2) if i % TW > 0]
    outer_pairs += [(i, i + 1) for i in range(1, n_blk, 2) if i % TW < TW - 1]

    if high == 2:
        swap = [(i, (i + TW) % n_blk) for i in range(n_blk)]
        beside = [(swap, swap, None)]
    else:
        down = [(i, i + TW) for i in range(n_blk - TW)]
        up = [(i + TW, i) for i in range(n_blk - TW)]
        beside = [(down, up, 1), (up, down, -1)]

    key, value = (pltpu.with_memory_space_constraint(a, pltpu.HBM) for a in (key, value))
    both, border, inner = pack(key, value)
    if is_small():
        far_live = blk_move(live, beside[0][0])
        far_live, query, both, border, inner = lax.optimization_barrier(
            (far_live, query, both, border, inner)
        )
        held = ((0, len(live), 0), (0, 0, 0), (0, 0, 0), (0, 0, 0))
        below = ((len(live), 0, 0), (0, 0, 0), (0, 0, 0), (0, 0, 0))
        live = lax.pad(live, 0, held) + lax.pad(far_live, 0, below)
        other_live = uly_swap(live)
        other_first = border
        far_bias = [biases(1, None, (live, other_live), "bias_beside")]
        border, far_bias = lax.optimization_barrier((border, far_bias))
        own_bias = biases(0, 0, (live, other_live), "bias_own")
    else:
        other_first = border
        own_live = lax.all_to_all(live, "uly", split_axis=1, concat_axis=0, tiled=True)
        own_bias = biases(0, 0, (own_live,), "bias_own")
        far_bias = [
            biases(1, height_step, (blk_move(own_live, there),), "bias_beside")
            for there, _, height_step in beside
        ]
    far_queries = [blk_move(query, there) for there, _, _ in beside]
    other_border = blk_move(other_first, outer_pairs)
    other_inner = blk_move(inner, outer_pairs)
    mate = blk_move(both, mate_pairs)
    own_halo = halo(border, inner)
    if is_small():
        token = blk_move(other_border[:TILE], mate_pairs)
        other_border, token = lax.optimization_barrier((other_border, token))
    other_halo = halo(other_border, other_inner)

    def attend_beside(at, after):
        return [
            attend(at, bias, block, blocks, beyond, True, "attend_beside", after)
            for block, bias in zip(far_queries, far_bias)
        ]

    blocks, beyond = (both, mate, other_border, other_inner), []
    made = [None, None]
    after = []
    if is_small():
        made[1] = attend_beside(1, [])
        own_halo, after = lax.optimization_barrier((own_halo, made[1]))
        after = after + [token]
    mate_halo = [blk_move(block, mate_pairs) for block in own_halo]
    beyond += [list(halos) for halos in zip(own_halo, mate_halo, other_halo)]
    if not is_small():
        made[1] = attend_beside(1, [])
    made[0] = attend_beside(0, after)
    returned = [
        [blk_move(part, back) for part, (_, back, _) in zip(made[at], beside)] for at in range(2)
    ]
    own = [
        attend(at, own_bias, query, blocks, beyond, False, "attend_own", [])
        for at in range(2)
    ]
    returned[1], own = lax.optimization_barrier((returned[1], own))
    out = None
    for at in (1, 0):
        out = combine(at, returned[at] + list(own[at]), len(beside), out)
    return out


def solution(mesh):
    return jax.shard_map(
        local,
        mesh=mesh,
        in_specs=(
            P(("uly", "blk"), None),
            P(("uly", "blk"), None),
            P(("uly", "blk"), None),
            P("uly", None, "blk", None),
        ),
        out_specs=P(("uly", "blk"), None),
        check_vma=False,
    )
```

```python
import functools

import jax
import jax.numpy as jnp
from jax import lax
from jax.experimental import pallas as pl
from jax.experimental.pallas import tpu as pltpu
from jax.sharding import PartitionSpec as P

HD = 128
HEADS = 8
TILE = 128
TW = 8
NEAR = 27
STEP = 4
COL = STEP * HD
C2 = HD ** (-0.5) * 1.4426950408889634
NONE = -1e30
STAT_ROWS = 8
TERMS = 3
VMEM = 20 * 2**20

ANYWHERE = pl.BlockSpec(memory_space=pl.ANY)
IN_SMEM = pl.BlockSpec(memory_space=pltpu.SMEM)
IN_VMEM = pl.BlockSpec(memory_space=pltpu.VMEM)


def is_small():
    return lax.axis_size("uly") == 2 and lax.axis_size("blk") == 2 * TW


def frame_of(at):
    if is_small():
        g = lax.axis_index("uly")
        return 1 - g if at == 0 else g
    return at


def slots_of(at):
    if is_small():
        outward = 1 - 2 * lax.axis_index("uly")
        return ((0, 0), (1, -outward), (2, outward)) if at == 0 else ((0, outward), (1, 0))
    return ((0, 0), (1, 1), (2, -1)) if at == 0 else ((0, -1), (1, 0), (3, 1))


def rows_of(at):
    return pl.ds(pl.multiple_of(frame_of(at) * TILE, TILE), TILE)


def pack_kernel(key, value, both, border, inner, sems):
    loads = {}
    for row, (at, half, source) in enumerate(((1, 0, key), (0, 0, key), (0, 1, value), (1, 1, value))):
        to = both.at[pl.ds(row * TILE, TILE)]
        loads[at, half] = pltpu.make_async_copy(source.at[rows_of(at)], to, sems.at[row])
    for at in range(2):
        for half in range(2):
            loads[at, half].start()
    for half in range(2):
        loads[0, half].wait()
    border[...] = both[TILE : 3 * TILE]
    for half in range(2):
        loads[1, half].wait()
    inner[:TILE] = both[:TILE]
    inner[TILE:] = both[3 * TILE :]


def pack(key, value):
    def rows(tiles):
        return jax.ShapeDtypeStruct((tiles * TILE, HEADS * HD), key.dtype)

    return pl.pallas_call(
        pack_kernel,
        out_shape=(rows(4), rows(2), rows(2)),
        in_specs=[pl.BlockSpec(memory_space=pltpu.HBM)] * 2,
        out_specs=(IN_VMEM,) * 3,
        scratch_shapes=[pltpu.SemaphoreType.DMA((4,))],
        compiler_params=pltpu.CompilerParams(vmem_limit_bytes=VMEM),
        cost_estimate=pl.CostEstimate(flops=0, bytes_accessed=2**21, transcendentals=0),
        name="pack_kv",
    )(key, value)


def bias_kernel(which, height_step, n_live, *refs):
    live, out = refs[:n_live], refs[n_live]
    g, s = lax.axis_index("uly"), lax.axis_index("blk")
    height = 2 * (s // TW) - 1 if height_step is None else height_step
    width = 1 - 2 * (s % 2)

    def is_live(at, head, offset):
        if is_small():
            held = HEADS // 2
            place = (which * held + head % held, 2 * g + frame_of(at), 0, offset)
            return jnp.where(g == head // held, live[0][place], live[1][place]) > 0
        return live[0][head, frame_of(at), 0, offset] > 0

    for at in range(2):
        for slot, frame_step in slots_of(at):
            for c, width_step in enumerate((0, width, -width)):
                offset = 9 * (frame_step + 1) + 3 * (height + 1) + width_step + 1
                for head in range(HEADS):
                    row = bias_row(at, slot, c, head)
                    bias = jnp.where(is_live(at, head, offset), 0.0, NONE)
                    out[row : row + 1] = jnp.full((1, HD), bias, jnp.float32)


def bias_row(at, slot, c, head):
    counts = [len(slots_of(part)) for part in range(2)]
    order = [number for number, _ in slots_of(at)].index(slot)
    return ((counts[0] * HEADS if at else 0) + head * counts[at] + order) * 3 + c


def biases(which, height_step, live, name):
    rows = sum(len(slots_of(at)) for at in range(2)) * HEADS * 3
    return pl.pallas_call(
        functools.partial(bias_kernel, which, height_step, len(live)),
        out_shape=jax.ShapeDtypeStruct((rows, HD), jnp.float32),
        in_specs=[IN_SMEM] * len(live),
        out_specs=IN_VMEM,
        compiler_params=pltpu.CompilerParams(vmem_limit_bytes=VMEM),
        name=name,
    )(*live)


def attend_kernel(at, places, travels, bias, query, *refs):
    out, stats_out = (refs[-1], None) if travels else refs[-2:]
    rows = rows_of(at)
    lane = lax.broadcasted_iota(jnp.int32, (TILE, HD), 1)

    cols = [slice(h * HD, (h + 1) * HD) for h in range(HEADS)]
    for step in range(HEADS // STEP):
        heads = range(step * STEP, (step + 1) * STEP)
        scores, highest = {}, {}
        for h in heads:
            q = query[rows, cols[h]]
            for block, (k_row, _, tiles) in enumerate(places):
                keys = refs[block][k_row : k_row + len(tiles) * TILE, cols[h]]
                score = lax.dot_general(
                    q, keys, (((1,), (1,)), ((), ())), preferred_element_type=jnp.float32
                )
                for i, t in enumerate(tiles):
                    part = score[:, i * TILE : (i + 1) * TILE]
                    row = bias_row(at, *t, h)
                    part = part + bias[row : row + 1]
                    scores[h, t] = part
                    highest[h] = jnp.maximum(highest[h], part) if h in highest else part
        top = {h: jnp.max(highest[h], axis=1, keepdims=True) for h in heads}
        shift = {h: top[h] * C2 for h in heads}
        mixed, sums = {}, {}
        for h in heads:
            for block, (_, v_row, tiles) in enumerate(places):
                weights = []
                for t in reversed(tiles):
                    w = jnp.exp2(scores[h, t] * C2 - shift[h])
                    sums[h] = sums[h] + w if h in sums else w
                    weights.append(w.astype(jnp.bfloat16))
                values = refs[block][v_row : v_row + len(tiles) * TILE, cols[h]]
                o = jnp.dot(
                    weights[0] if len(weights) == 1 else jnp.concatenate(weights, axis=1),
                    values,
                    preferred_element_type=jnp.float32,
                )
                mixed[h] = mixed[h] + o if h in mixed else o
        total = {h: jnp.sum(sums[h], axis=1, keepdims=True) for h in heads}
        stats = jnp.zeros((TILE, HD), jnp.float32)
        for i, h in enumerate(heads):
            if travels:
                any_live = top[h] > 0.5 * NONE
                total[h] = jnp.where(any_live, total[h], 0.0)
                mixed[h] = mixed[h] * jnp.where(any_live, 1.0 / total[h], 0.0)
            out[:TILE, cols[h]] = mixed[h].astype(out.dtype)
            stats = jnp.where(lane == i, top[h], stats)
            stats = jnp.where(lane == STEP + i, total[h], stats)
        stats = jnp.transpose(stats)[:STAT_ROWS]
        if travels:
            for term in range(TERMS):
                rounded = stats.astype(jnp.bfloat16)
                out[TILE:, cols[heads[term]]] = rounded
                stats = stats - rounded.astype(jnp.float32)
            out[TILE:, cols[heads[TERMS]]] = jnp.zeros((STAT_ROWS, HD), jnp.bfloat16)
        else:
            stats_out[step * STAT_ROWS : (step + 1) * STAT_ROWS] = stats


def attend(at, bias, query, both, beyond, travels, name, after):
    blocks = list(both)
    places = [(0, 2 * TILE, ((1, c), (0, c))) for c in range(2)]
    places += [(0, TILE, ((slot, 2),)) for slot in range(2)]
    for slot, _ in slots_of(at)[2:]:
        blocks += beyond[slot - 2]
        places += [(0, TILE, ((slot, c),)) for c in range(3)]
    pairs = sum(len(tiles) for _, _, tiles in places) * HEADS
    steps = HEADS // STEP
    if travels:
        out_shape = jax.ShapeDtypeStruct((TILE + STAT_ROWS, HEADS * HD), jnp.bfloat16)
    else:
        out_shape = (
            jax.ShapeDtypeStruct((TILE, HEADS * HD), jnp.float32),
            jax.ShapeDtypeStruct((steps * STAT_ROWS, HD), jnp.float32),
        )
    return pl.pallas_call(
        functools.partial(attend_kernel, at, places, travels),
        out_shape=out_shape,
        in_specs=[IN_VMEM] * (2 + len(blocks)) + [ANYWHERE] * len(after),
        out_specs=IN_VMEM if travels else (IN_VMEM, IN_VMEM),
        compiler_params=pltpu.CompilerParams(vmem_limit_bytes=VMEM),
        cost_estimate=pl.CostEstimate(
            flops=4 * pairs * TILE * TILE * HD,
            bytes_accessed=(pairs // HEADS + 2) * 2 * TILE * HEADS * HD * 2,
            transcendentals=pairs * TILE * TILE,
        ),
        name=name,
    )(bias, query, *blocks, *after)


def split_stats(per_step):
    tops = jnp.concatenate([stats[:STEP] for stats in per_step], axis=0)
    totals = jnp.concatenate([stats[STEP : 2 * STEP] for stats in per_step], axis=0)
    return tops, totals


def own_stats(ref):
    steps = range(HEADS // STEP)
    return split_stats([ref[step * STAT_ROWS : (step + 1) * STAT_ROWS] for step in steps])


def travelled_stats(ref):
    per_step = []
    for step in range(HEADS // STEP):
        first = step * COL
        terms = [ref[TILE:, first + HD * t : first + HD * (t + 1)] for t in range(TERMS)]
        per_step.append(sum(term.astype(jnp.float32) for term in terms))
    return split_stats(per_step)


def combine_kernel(at, n_more, *refs):
    out, made, sem = refs[-3:]
    travelled, (mine, stats) = refs[:n_more], refs[n_more : n_more + 2]
    top, total = own_stats(stats)
    more = []
    best = top
    for m in range(n_more):
        top2, total2 = travelled_stats(travelled[m])
        top2 = jnp.where(total2 > 0.0, top2, NONE)
        more.append((top2, total2))
        best = jnp.maximum(best, top2)
    own = jnp.exp2((top - best) * C2)
    weights = [own]
    whole = total * own
    for top2, total2 in more:
        w = jnp.exp2((top2 - best) * C2) * total2
        weights.append(w)
        whole = whole + w
    inverse = 1.0 / whole
    weights = [w * inverse for w in weights]
    fill = TILE - HEADS * len(weights)
    columns = jnp.transpose(
        jnp.concatenate(weights + [jnp.zeros((fill, HD), jnp.float32)], axis=0)
    )
    for h in range(HEADS):
        cols = slice(h * HD, (h + 1) * HD)
        value = mine[:, cols] * columns[:, h : h + 1]
        for m in range(n_more):
            c = (m + 1) * HEADS + h
            value = value + travelled[m][:TILE, cols].astype(jnp.float32) * columns[:, c : c + 1]
        made[:, cols] = value.astype(made.dtype)
    copy = pltpu.make_async_copy(made, out.at[rows_of(at)], sem)
    copy.start()
    copy.wait()


def combine(at, parts, n_more, into=None):
    specs = [IN_VMEM] * len(parts)
    extra, aliases = [], {}
    if into is not None:
        specs.append(ANYWHERE)
        extra, aliases = [into], {len(parts): 0}
    return pl.pallas_call(
        functools.partial(combine_kernel, at, n_more),
        out_shape=jax.ShapeDtypeStruct((2 * TILE, HEADS * HD), jnp.bfloat16),
        in_specs=specs,
        out_specs=ANYWHERE,
        scratch_shapes=[
            pltpu.VMEM((TILE, HEADS * HD), jnp.bfloat16),
            pltpu.SemaphoreType.DMA,
        ],
        input_output_aliases=aliases,
        compiler_params=pltpu.CompilerParams(vmem_limit_bytes=VMEM),
        name="combine",
    )(*parts, *extra)


def local(query, key, value, live):
    n_uly, n_blk = lax.axis_size("uly"), lax.axis_size("blk")
    high = n_blk // TW

    def blk_move(block, pairs):
        return lax.ppermute(block, "blk", pairs)

    def uly_shift(block, distance):
        pairs = [(i, i + distance) for i in range(n_uly) if 0 <= i + distance < n_uly]
        return lax.ppermute(block, "uly", pairs)

    def uly_swap(block):
        return lax.ppermute(block, "uly", [(0, 1), (1, 0)])

    def halo(first, second):
        if is_small():
            return [uly_swap(first)]
        return [uly_shift(second, 1), uly_shift(first, -1)]

    mate_pairs = [(i, i ^ 1) for i in range(n_blk)]
    outer_pairs = [(i, i - 1) for i in range(0, n_blk, 2) if i % TW > 0]
    outer_pairs += [(i, i + 1) for i in range(1, n_blk, 2) if i % TW < TW - 1]

    if high == 2:
        swap = [(i, (i + TW) % n_blk) for i in range(n_blk)]
        beside = [(swap, swap, None)]
    else:
        down = [(i, i + TW) for i in range(n_blk - TW)]
        up = [(i + TW, i) for i in range(n_blk - TW)]
        beside = [(down, up, 1), (up, down, -1)]

    key, value = (pltpu.with_memory_space_constraint(a, pltpu.HBM) for a in (key, value))
    both, border, inner = pack(key, value)
    if is_small():
        far_live = blk_move(live, beside[0][0])
        far_live, query, both, border, inner = lax.optimization_barrier(
            (far_live, query, both, border, inner)
        )
        held = ((0, len(live), 0), (0, 0, 0), (0, 0, 0), (0, 0, 0))
        below = ((len(live), 0, 0), (0, 0, 0), (0, 0, 0), (0, 0, 0))
        live = lax.pad(live, 0, held) + lax.pad(far_live, 0, below)
        other_live = uly_swap(live)
        other_first = border
        border, other_live = lax.optimization_barrier((border, other_live))
        far_bias = [biases(1, None, (live, other_live), "bias_beside")]
        own_bias = biases(0, 0, (live, other_live), "bias_own")
    else:
        other_first = border
        own_live = lax.all_to_all(live, "uly", split_axis=1, concat_axis=0, tiled=True)
        own_bias = biases(0, 0, (own_live,), "bias_own")
        far_bias = [
            biases(1, height_step, (blk_move(own_live, there),), "bias_beside")
            for there, _, height_step in beside
        ]
    far_queries = [blk_move(query, there) for there, _, _ in beside]
    other_border = blk_move(other_first, outer_pairs)
    other_inner = blk_move(inner, outer_pairs)
    mate = blk_move(both, mate_pairs)
    own_halo = halo(border, inner)
    if is_small():
        other_border, far_bias = lax.optimization_barrier((other_border, far_bias))
        token = blk_move(other_border[:TILE], mate_pairs)
        other_border, token = lax.optimization_barrier((other_border, token))
    other_halo = halo(other_border, other_inner)

    def attend_beside(at, after):
        return [
            attend(at, bias, block, blocks, beyond, True, "attend_beside", after)
            for block, bias in zip(far_queries, far_bias)
        ]

    blocks, beyond = (both, mate, other_border, other_inner), []
    made = [None, None]
    after = []
    if is_small():
        made[1] = attend_beside(1, [])
        own_halo, after = lax.optimization_barrier((own_halo, made[1]))
        after = after + [token]
    mate_halo = [blk_move(block, mate_pairs) for block in own_halo]
    beyond += [list(halos) for halos in zip(own_halo, mate_halo, other_halo)]
    if not is_small():
        made[1] = attend_beside(1, [])
    made[0] = attend_beside(0, after)
    returned = [
        [blk_move(part, back) for part, (_, back, _) in zip(made[at], beside)] for at in range(2)
    ]
    own = [
        attend(at, own_bias, query, blocks, beyond, False, "attend_own", [])
        for at in range(2)
    ]
    returned[1], own = lax.optimization_barrier((returned[1], own))
    out = None
    for at in (1, 0):
        out = combine(at, returned[at] + list(own[at]), len(beside), out)
    return out


def solution(mesh):
    return jax.shard_map(
        local,
        mesh=mesh,
        in_specs=(
            P(("uly", "blk"), None),
            P(("uly", "blk"), None),
            P(("uly", "blk"), None),
            P("uly", None, "blk", None),
        ),
        out_specs=P(("uly", "blk"), None),
        check_vma=False,
    )
```

```python
import functools

import jax
import jax.numpy as jnp
from jax import lax
from jax.experimental import pallas as pl
from jax.experimental.pallas import tpu as pltpu
from jax.sharding import PartitionSpec as P

HD = 128
HEADS = 8
TILE = 128
TW = 8
NEAR = 27
STEP = 4
COL = STEP * HD
C2 = HD ** (-0.5) * 1.4426950408889634
NONE = -1e30
STAT_ROWS = 16
TERMS = 3
VMEM = 20 * 2**20

ANYWHERE = pl.BlockSpec(memory_space=pl.ANY)
IN_SMEM = pl.BlockSpec(memory_space=pltpu.SMEM)
IN_VMEM = pl.BlockSpec(memory_space=pltpu.VMEM)


def is_small():
    return lax.axis_size("uly") == 2 and lax.axis_size("blk") == 2 * TW


def frame_of(at):
    if is_small():
        g = lax.axis_index("uly")
        return 1 - g if at == 0 else g
    return at


def slots_of(at):
    if is_small():
        outward = 1 - 2 * lax.axis_index("uly")
        return ((0, 0), (1, -outward), (2, outward)) if at == 0 else ((0, outward), (1, 0))
    return ((0, 0), (1, 1), (2, -1)) if at == 0 else ((0, -1), (1, 0), (3, 1))


def rows_of(at):
    return pl.ds(pl.multiple_of(frame_of(at) * TILE, TILE), TILE)


def pack_kernel(key, value, both, border, inner, sems):
    loads = {}
    for row, (at, half, source) in enumerate(((1, 0, key), (0, 0, key), (0, 1, value), (1, 1, value))):
        to = both.at[pl.ds(row * TILE, TILE)]
        loads[at, half] = pltpu.make_async_copy(source.at[rows_of(at)], to, sems.at[row])
    for at in range(2):
        for half in range(2):
            loads[at, half].start()
    for half in range(2):
        loads[0, half].wait()
    border[...] = both[TILE : 3 * TILE]
    for half in range(2):
        loads[1, half].wait()
    inner[:TILE] = both[:TILE]
    inner[TILE:] = both[3 * TILE :]


def pack(key, value):
    def rows(tiles):
        return jax.ShapeDtypeStruct((tiles * TILE, HEADS * HD), key.dtype)

    return pl.pallas_call(
        pack_kernel,
        out_shape=(rows(4), rows(2), rows(2)),
        in_specs=[pl.BlockSpec(memory_space=pltpu.HBM)] * 2,
        out_specs=(IN_VMEM,) * 3,
        scratch_shapes=[pltpu.SemaphoreType.DMA((4,))],
        compiler_params=pltpu.CompilerParams(vmem_limit_bytes=VMEM),
        cost_estimate=pl.CostEstimate(flops=0, bytes_accessed=2**21, transcendentals=0),
        name="pack_kv",
    )(key, value)


def bias_kernel(which, height_step, n_live, *refs):
    live, out = refs[:n_live], refs[n_live]
    g, s = lax.axis_index("uly"), lax.axis_index("blk")
    height = 2 * (s // TW) - 1 if height_step is None else height_step
    width = 1 - 2 * (s % 2)

    def is_live(at, head, offset):
        if is_small():
            held = HEADS // 2
            place = (which * held + head % held, 2 * g + frame_of(at), 0, offset)
            return jnp.where(g == head // held, live[0][place], live[1][place]) > 0
        return live[0][head, frame_of(at), 0, offset] > 0

    for at in range(2):
        for slot, frame_step in slots_of(at):
            for c, width_step in enumerate((0, width, -width)):
                offset = 9 * (frame_step + 1) + 3 * (height + 1) + width_step + 1
                for head in range(HEADS):
                    row = bias_row(at, slot, c, head)
                    bias = jnp.where(is_live(at, head, offset), 0.0, NONE)
                    out[row : row + 1] = jnp.full((1, HD), bias, jnp.float32)


def bias_row(at, slot, c, head):
    counts = [len(slots_of(part)) for part in range(2)]
    order = [number for number, _ in slots_of(at)].index(slot)
    return ((counts[0] * HEADS if at else 0) + head * counts[at] + order) * 3 + c


def biases(which, height_step, live, name):
    rows = sum(len(slots_of(at)) for at in range(2)) * HEADS * 3
    return pl.pallas_call(
        functools.partial(bias_kernel, which, height_step, len(live)),
        out_shape=jax.ShapeDtypeStruct((rows, HD), jnp.float32),
        in_specs=[IN_SMEM] * len(live),
        out_specs=IN_VMEM,
        compiler_params=pltpu.CompilerParams(vmem_limit_bytes=VMEM),
        name=name,
    )(*live)


def attend_kernel(at, places, travels, bias, query, *refs):
    out, stats_out = (refs[-1], None) if travels else refs[-2:]
    rows = rows_of(at)
    lane = lax.broadcasted_iota(jnp.int32, (TILE, HD), 1)

    cols = [slice(h * HD, (h + 1) * HD) for h in range(HEADS)]
    for step in range(HEADS // STEP):
        heads = range(step * STEP, (step + 1) * STEP)
        scores, highest = {}, {}
        for h in heads:
            q = query[rows, cols[h]]
            for block, (k_row, _, tiles) in enumerate(places):
                keys = refs[block][k_row : k_row + len(tiles) * TILE, cols[h]]
                score = lax.dot_general(
                    q, keys, (((1,), (1,)), ((), ())), preferred_element_type=jnp.float32
                )
                for i, t in enumerate(tiles):
                    part = score[:, i * TILE : (i + 1) * TILE]
                    row = bias_row(at, *t, h)
                    part = part + bias[row : row + 1]
                    scores[h, t] = part
                    highest[h] = jnp.maximum(highest[h], part) if h in highest else part
        top = {h: jnp.max(highest[h], axis=1, keepdims=True) for h in heads}
        shift = {h: top[h] * C2 for h in heads}
        mixed, sums = {}, {}
        for h in heads:
            for block, (_, v_row, tiles) in enumerate(places):
                weights = []
                for t in reversed(tiles):
                    w = jnp.exp2(scores[h, t] * C2 - shift[h])
                    sums[h] = sums[h] + w if h in sums else w
                    weights.append(w.astype(jnp.bfloat16))
                values = refs[block][v_row : v_row + len(tiles) * TILE, cols[h]]
                o = jnp.dot(
                    weights[0] if len(weights) == 1 else jnp.concatenate(weights, axis=1),
                    values,
                    preferred_element_type=jnp.float32,
                )
                mixed[h] = mixed[h] + o if h in mixed else o
        total = {h: jnp.sum(sums[h], axis=1, keepdims=True) for h in heads}
        stats = jnp.zeros((TILE, HD), jnp.float32)
        for i, h in enumerate(heads):
            if travels:
                any_live = top[h] > 0.5 * NONE
                total[h] = jnp.where(any_live, total[h], 0.0)
                mixed[h] = mixed[h] * jnp.where(any_live, 1.0 / total[h], 0.0)
            out[:TILE, cols[h]] = mixed[h].astype(out.dtype)
            stats = jnp.where(lane == i, top[h], stats)
            stats = jnp.where(lane == STEP + i, total[h], stats)
        stats = jnp.transpose(stats)[:STAT_ROWS]
        if travels:
            for term in range(TERMS):
                rounded = stats.astype(jnp.bfloat16)
                out[TILE:, cols[heads[term]]] = rounded
                stats = stats - rounded.astype(jnp.float32)
            out[TILE:, cols[heads[TERMS]]] = jnp.zeros((STAT_ROWS, HD), jnp.bfloat16)
        else:
            stats_out[step * STAT_ROWS : (step + 1) * STAT_ROWS] = stats


def attend(at, bias, query, both, beyond, travels, name, after):
    blocks = list(both)
    places = [(0, 2 * TILE, ((1, c), (0, c))) for c in range(2)]
    places += [(0, TILE, ((slot, 2),)) for slot in range(2)]
    for slot, _ in slots_of(at)[2:]:
        blocks += beyond[slot - 2]
        places += [(0, TILE, ((slot, c),)) for c in range(3)]
    pairs = sum(len(tiles) for _, _, tiles in places) * HEADS
    steps = HEADS // STEP
    if travels:
        out_shape = jax.ShapeDtypeStruct((TILE + STAT_ROWS, HEADS * HD), jnp.bfloat16)
    else:
        out_shape = (
            jax.ShapeDtypeStruct((TILE, HEADS * HD), jnp.float32),
            jax.ShapeDtypeStruct((steps * STAT_ROWS, HD), jnp.float32),
        )
    return pl.pallas_call(
        functools.partial(attend_kernel, at, places, travels),
        out_shape=out_shape,
        in_specs=[IN_VMEM] * (2 + len(blocks)) + [ANYWHERE] * len(after),
        out_specs=IN_VMEM if travels else (IN_VMEM, IN_VMEM),
        compiler_params=pltpu.CompilerParams(vmem_limit_bytes=VMEM),
        cost_estimate=pl.CostEstimate(
            flops=4 * pairs * TILE * TILE * HD,
            bytes_accessed=(pairs // HEADS + 2) * 2 * TILE * HEADS * HD * 2,
            transcendentals=pairs * TILE * TILE,
        ),
        name=name,
    )(bias, query, *blocks, *after)


def split_stats(per_step):
    tops = jnp.concatenate([stats[:STEP] for stats in per_step], axis=0)
    totals = jnp.concatenate([stats[STEP : 2 * STEP] for stats in per_step], axis=0)
    return tops, totals


def own_stats(ref):
    steps = range(HEADS // STEP)
    return split_stats([ref[step * STAT_ROWS : (step + 1) * STAT_ROWS] for step in steps])


def travelled_stats(ref):
    per_step = []
    for step in range(HEADS // STEP):
        first = step * COL
        terms = [ref[TILE:, first + HD * t : first + HD * (t + 1)] for t in range(TERMS)]
        per_step.append(sum(term.astype(jnp.float32) for term in terms))
    return split_stats(per_step)


def combine_kernel(at, n_more, *refs):
    out, made, sem = refs[-3:]
    travelled, (mine, stats) = refs[:n_more], refs[n_more : n_more + 2]
    top, total = own_stats(stats)
    more = []
    best = top
    for m in range(n_more):
        top2, total2 = travelled_stats(travelled[m])
        top2 = jnp.where(total2 > 0.0, top2, NONE)
        more.append((top2, total2))
        best = jnp.maximum(best, top2)
    own = jnp.exp2((top - best) * C2)
    weights = [own]
    whole = total * own
    for top2, total2 in more:
        w = jnp.exp2((top2 - best) * C2) * total2
        weights.append(w)
        whole = whole + w
    inverse = 1.0 / whole
    weights = [w * inverse for w in weights]
    fill = TILE - HEADS * len(weights)
    columns = jnp.transpose(
        jnp.concatenate(weights + [jnp.zeros((fill, HD), jnp.float32)], axis=0)
    )
    for h in range(HEADS):
        cols = slice(h * HD, (h + 1) * HD)
        value = mine[:, cols] * columns[:, h : h + 1]
        for m in range(n_more):
            c = (m + 1) * HEADS + h
            value = value + travelled[m][:TILE, cols].astype(jnp.float32) * columns[:, c : c + 1]
        made[:, cols] = value.astype(made.dtype)
    copy = pltpu.make_async_copy(made, out.at[rows_of(at)], sem)
    copy.start()
    copy.wait()


def combine(at, parts, n_more, into=None):
    specs = [IN_VMEM] * len(parts)
    extra, aliases = [], {}
    if into is not None:
        specs.append(ANYWHERE)
        extra, aliases = [into], {len(parts): 0}
    return pl.pallas_call(
        functools.partial(combine_kernel, at, n_more),
        out_shape=jax.ShapeDtypeStruct((2 * TILE, HEADS * HD), jnp.bfloat16),
        in_specs=specs,
        out_specs=ANYWHERE,
        scratch_shapes=[
            pltpu.VMEM((TILE, HEADS * HD), jnp.bfloat16),
            pltpu.SemaphoreType.DMA,
        ],
        input_output_aliases=aliases,
        compiler_params=pltpu.CompilerParams(vmem_limit_bytes=VMEM),
        name="combine",
    )(*parts, *extra)


def local(query, key, value, live):
    n_uly, n_blk = lax.axis_size("uly"), lax.axis_size("blk")
    high = n_blk // TW

    def blk_move(block, pairs):
        return lax.ppermute(block, "blk", pairs)

    def uly_shift(block, distance):
        pairs = [(i, i + distance) for i in range(n_uly) if 0 <= i + distance < n_uly]
        return lax.ppermute(block, "uly", pairs)

    def uly_swap(block):
        return lax.ppermute(block, "uly", [(0, 1), (1, 0)])

    def halo(first, second):
        if is_small():
            return [uly_swap(first)]
        return [uly_shift(second, 1), uly_shift(first, -1)]

    mate_pairs = [(i, i ^ 1) for i in range(n_blk)]
    outer_pairs = [(i, i - 1) for i in range(0, n_blk, 2) if i % TW > 0]
    outer_pairs += [(i, i + 1) for i in range(1, n_blk, 2) if i % TW < TW - 1]

    if high == 2:
        swap = [(i, (i + TW) % n_blk) for i in range(n_blk)]
        beside = [(swap, swap, None)]
    else:
        down = [(i, i + TW) for i in range(n_blk - TW)]
        up = [(i + TW, i) for i in range(n_blk - TW)]
        beside = [(down, up, 1), (up, down, -1)]

    key, value = (pltpu.with_memory_space_constraint(a, pltpu.HBM) for a in (key, value))
    both, border, inner = pack(key, value)
    if is_small():
        far_live = blk_move(live, beside[0][0])
        far_live, query, both, border, inner = lax.optimization_barrier(
            (far_live, query, both, border, inner)
        )
        held = ((0, len(live), 0), (0, 0, 0), (0, 0, 0), (0, 0, 0))
        below = ((len(live), 0, 0), (0, 0, 0), (0, 0, 0), (0, 0, 0))
        live = lax.pad(live, 0, held) + lax.pad(far_live, 0, below)
        other_live = uly_swap(live)
        other_first = border
        border, other_live = lax.optimization_barrier((border, other_live))
        far_bias = [biases(1, None, (live, other_live), "bias_beside")]
        own_bias = biases(0, 0, (live, other_live), "bias_own")
    else:
        other_first = border
        own_live = lax.all_to_all(live, "uly", split_axis=1, concat_axis=0, tiled=True)
        own_bias = biases(0, 0, (own_live,), "bias_own")
        far_bias = [
            biases(1, height_step, (blk_move(own_live, there),), "bias_beside")
            for there, _, height_step in beside
        ]
    far_queries = [blk_move(query, there) for there, _, _ in beside]
    other_border = blk_move(other_first, outer_pairs)
    other_inner = blk_move(inner, outer_pairs)
    mate = blk_move(both, mate_pairs)
    own_halo = halo(border, inner)
    if is_small():
        other_border, far_bias = lax.optimization_barrier((other_border, far_bias))
        token = blk_move(other_border[:TILE], mate_pairs)
        other_border, token = lax.optimization_barrier((other_border, token))
    other_halo = halo(other_border, other_inner)

    def attend_beside(at, after):
        return [
            attend(at, bias, block, blocks, beyond, True, "attend_beside", after)
            for block, bias in zip(far_queries, far_bias)
        ]

    blocks, beyond = (both, mate, other_border, other_inner), []
    made = [None, None]
    after = []
    if is_small():
        made[1] = attend_beside(1, [])
        own_halo, after = lax.optimization_barrier((own_halo, made[1]))
        after = after + [token]
    mate_halo = [blk_move(block, mate_pairs) for block in own_halo]
    beyond += [list(halos) for halos in zip(own_halo, mate_halo, other_halo)]
    if not is_small():
        made[1] = attend_beside(1, [])
    made[0] = attend_beside(0, after)
    returned = [
        [blk_move(part, back) for part, (_, back, _) in zip(made[at], beside)] for at in range(2)
    ]
    own = [
        attend(at, own_bias, query, blocks, beyond, False, "attend_own", [])
        for at in range(2)
    ]
    returned[1], own = lax.optimization_barrier((returned[1], own))
    out = None
    for at in (1, 0):
        out = combine(at, returned[at] + list(own[at]), len(beside), out)
    return out


def solution(mesh):
    return jax.shard_map(
        local,
        mesh=mesh,
        in_specs=(
            P(("uly", "blk"), None),
            P(("uly", "blk"), None),
            P(("uly", "blk"), None),
            P("uly", None, "blk", None),
        ),
        out_specs=P(("uly", "blk"), None),
        check_vma=False,
    )
```

```python
import functools

import jax
import jax.numpy as jnp
from jax import lax
from jax.experimental import pallas as pl
from jax.experimental.pallas import tpu as pltpu
from jax.sharding import PartitionSpec as P

HD = 128
HEADS = 8
TILE = 128
TW = 8
NEAR = 27
STEP = 4
COL = STEP * HD
C2 = HD ** (-0.5) * 1.4426950408889634
NONE = -1e30
STAT_ROWS = 8
TERMS = 3
VMEM = 20 * 2**20

ANYWHERE = pl.BlockSpec(memory_space=pl.ANY)
IN_SMEM = pl.BlockSpec(memory_space=pltpu.SMEM)
IN_VMEM = pl.BlockSpec(memory_space=pltpu.VMEM)


def is_small():
    return lax.axis_size("uly") == 2 and lax.axis_size("blk") == 2 * TW


def frame_of(at):
    if is_small():
        g = lax.axis_index("uly")
        return 1 - g if at == 0 else g
    return at


def slots_of(at):
    if is_small():
        outward = 1 - 2 * lax.axis_index("uly")
        return ((0, 0), (1, -outward), (2, outward)) if at == 0 else ((0, outward), (1, 0))
    return ((0, 0), (1, 1), (2, -1)) if at == 0 else ((0, -1), (1, 0), (3, 1))


def rows_of(at):
    return pl.ds(pl.multiple_of(frame_of(at) * TILE, TILE), TILE)


def pack_kernel(key, value, both, border, inner, sems):
    loads = {}
    for row, (at, half, source) in enumerate(((1, 0, key), (0, 0, key), (0, 1, value), (1, 1, value))):
        to = both.at[pl.ds(row * TILE, TILE)]
        loads[at, half] = pltpu.make_async_copy(source.at[rows_of(at)], to, sems.at[row])
    for at in range(2):
        for half in range(2):
            loads[at, half].start()
    for half in range(2):
        loads[0, half].wait()
    border[...] = both[TILE : 3 * TILE]
    for half in range(2):
        loads[1, half].wait()
    inner[:TILE] = both[:TILE]
    inner[TILE:] = both[3 * TILE :]


def pack(key, value):
    def rows(tiles):
        return jax.ShapeDtypeStruct((tiles * TILE, HEADS * HD), key.dtype)

    return pl.pallas_call(
        pack_kernel,
        out_shape=(rows(4), rows(2), rows(2)),
        in_specs=[pl.BlockSpec(memory_space=pltpu.HBM)] * 2,
        out_specs=(IN_VMEM,) * 3,
        scratch_shapes=[pltpu.SemaphoreType.DMA((4,))],
        compiler_params=pltpu.CompilerParams(vmem_limit_bytes=VMEM),
        cost_estimate=pl.CostEstimate(flops=0, bytes_accessed=2**21, transcendentals=0),
        name="pack_kv",
    )(key, value)


def bias_kernel(which, height_step, n_live, *refs):
    live, out = refs[:n_live], refs[n_live]
    g, s = lax.axis_index("uly"), lax.axis_index("blk")
    height = 2 * (s // TW) - 1 if height_step is None else height_step
    width = 1 - 2 * (s % 2)

    def is_live(at, head, offset):
        if is_small():
            held = HEADS // 2
            place = (which * held + head % held, 2 * g + frame_of(at), 0, offset)
            return jnp.where(g == head // held, live[0][place], live[1][place]) > 0
        return live[0][head, frame_of(at), 0, offset] > 0

    for at in range(2):
        for slot, frame_step in slots_of(at):
            for c, width_step in enumerate((0, width, -width)):
                offset = 9 * (frame_step + 1) + 3 * (height + 1) + width_step + 1
                for head in range(HEADS):
                    row = bias_row(at, slot, c, head)
                    bias = jnp.where(is_live(at, head, offset), 0.0, NONE)
                    out[row : row + 1] = jnp.full((1, HD), bias, jnp.float32)


def bias_row(at, slot, c, head):
    counts = [len(slots_of(part)) for part in range(2)]
    order = [number for number, _ in slots_of(at)].index(slot)
    return ((counts[0] * HEADS if at else 0) + head * counts[at] + order) * 3 + c


def biases(which, height_step, live, name):
    rows = sum(len(slots_of(at)) for at in range(2)) * HEADS * 3
    return pl.pallas_call(
        functools.partial(bias_kernel, which, height_step, len(live)),
        out_shape=jax.ShapeDtypeStruct((rows, HD), jnp.float32),
        in_specs=[IN_SMEM] * len(live),
        out_specs=IN_VMEM,
        compiler_params=pltpu.CompilerParams(vmem_limit_bytes=VMEM),
        name=name,
    )(*live)


def attend_kernel(at, places, travels, bias, query, *refs):
    out, stats_out = (refs[-1], None) if travels else refs[-2:]
    rows = rows_of(at)
    lane = lax.broadcasted_iota(jnp.int32, (TILE, HD), 1)

    cols = [slice(h * HD, (h + 1) * HD) for h in range(HEADS)]
    for step in range(HEADS // STEP):
        heads = range(step * STEP, (step + 1) * STEP)
        scores, highest = {}, {}
        for h in heads:
            q = query[rows, cols[h]]
            for block, (k_row, _, tiles) in enumerate(places):
                keys = refs[block][k_row : k_row + len(tiles) * TILE, cols[h]]
                score = lax.dot_general(
                    q, keys, (((1,), (1,)), ((), ())), preferred_element_type=jnp.float32
                )
                for i, t in enumerate(tiles):
                    part = score[:, i * TILE : (i + 1) * TILE]
                    row = bias_row(at, *t, h)
                    part = part + bias[row : row + 1]
                    scores[h, t] = part
                    highest[h] = jnp.maximum(highest[h], part) if h in highest else part
        top = {h: jnp.max(highest[h], axis=1, keepdims=True) for h in heads}
        shift = {h: top[h] * C2 for h in heads}
        mixed, sums = {}, {}
        for h in heads:
            for block, (_, v_row, tiles) in enumerate(places):
                weights = []
                for t in reversed(tiles):
                    w = jnp.exp2(scores[h, t] * C2 - shift[h])
                    sums[h] = sums[h] + w if h in sums else w
                    weights.append(w.astype(jnp.bfloat16))
                values = refs[block][v_row : v_row + len(tiles) * TILE, cols[h]]
                o = jnp.dot(
                    weights[0] if len(weights) == 1 else jnp.concatenate(weights, axis=1),
                    values,
                    preferred_element_type=jnp.float32,
                )
                mixed[h] = mixed[h] + o if h in mixed else o
        total = {h: jnp.sum(sums[h], axis=1, keepdims=True) for h in heads}
        stats = jnp.zeros((TILE, HD), jnp.float32)
        for i, h in enumerate(heads):
            if travels:
                any_live = top[h] > 0.5 * NONE
                total[h] = jnp.where(any_live, total[h], 0.0)
                mixed[h] = mixed[h] * jnp.where(any_live, 1.0 / total[h], 0.0)
            out[:TILE, cols[h]] = mixed[h].astype(out.dtype)
            stats = jnp.where(lane == i, top[h], stats)
            stats = jnp.where(lane == STEP + i, total[h], stats)
        stats = jnp.transpose(stats)[:STAT_ROWS]
        if travels:
            for term in range(TERMS):
                rounded = stats.astype(jnp.bfloat16)
                out[TILE:, cols[heads[term]]] = rounded
                stats = stats - rounded.astype(jnp.float32)
            out[TILE:, cols[heads[TERMS]]] = jnp.zeros((STAT_ROWS, HD), jnp.bfloat16)
        else:
            stats_out[step * STAT_ROWS : (step + 1) * STAT_ROWS] = stats


def attend(at, bias, query, both, beyond, travels, name, after):
    blocks = list(both)
    places = [(0, 2 * TILE, ((1, c), (0, c))) for c in range(2)]
    places += [(0, TILE, ((slot, 2),)) for slot in range(2)]
    for slot, _ in slots_of(at)[2:]:
        blocks += beyond[slot - 2]
        places += [(0, TILE, ((slot, c),)) for c in range(3)]
    pairs = sum(len(tiles) for _, _, tiles in places) * HEADS
    steps = HEADS // STEP
    if travels:
        out_shape = jax.ShapeDtypeStruct((TILE + STAT_ROWS, HEADS * HD), jnp.bfloat16)
    else:
        out_shape = (
            jax.ShapeDtypeStruct((TILE, HEADS * HD), jnp.float32),
            jax.ShapeDtypeStruct((steps * STAT_ROWS, HD), jnp.float32),
        )
    return pl.pallas_call(
        functools.partial(attend_kernel, at, places, travels),
        out_shape=out_shape,
        in_specs=[IN_VMEM] * (2 + len(blocks)) + [ANYWHERE] * len(after),
        out_specs=IN_VMEM if travels else (IN_VMEM, IN_VMEM),
        compiler_params=pltpu.CompilerParams(vmem_limit_bytes=VMEM),
        cost_estimate=pl.CostEstimate(
            flops=4 * pairs * TILE * TILE * HD,
            bytes_accessed=(pairs // HEADS + 2) * 2 * TILE * HEADS * HD * 2,
            transcendentals=pairs * TILE * TILE,
        ),
        name=name,
    )(bias, query, *blocks, *after)


def split_stats(per_step):
    tops = jnp.concatenate([stats[:STEP] for stats in per_step], axis=0)
    totals = jnp.concatenate([stats[STEP : 2 * STEP] for stats in per_step], axis=0)
    return tops, totals


def own_stats(ref):
    steps = range(HEADS // STEP)
    return split_stats([ref[step * STAT_ROWS : (step + 1) * STAT_ROWS] for step in steps])


def travelled_stats(ref):
    per_step = []
    for step in range(HEADS // STEP):
        first = step * COL
        terms = [ref[TILE:, first + HD * t : first + HD * (t + 1)] for t in range(TERMS)]
        per_step.append(sum(term.astype(jnp.float32) for term in terms))
    return split_stats(per_step)


def combine_kernel(at, n_more, *refs):
    out, made, sem = refs[-3:]
    travelled, (mine, stats) = refs[:n_more], refs[n_more : n_more + 2]
    top, total = own_stats(stats)
    more = []
    best = top
    for m in range(n_more):
        top2, total2 = travelled_stats(travelled[m])
        top2 = jnp.where(total2 > 0.0, top2, NONE)
        more.append((top2, total2))
        best = jnp.maximum(best, top2)
    own = jnp.exp2((top - best) * C2)
    weights = [own]
    whole = total * own
    for top2, total2 in more:
        w = jnp.exp2((top2 - best) * C2) * total2
        weights.append(w)
        whole = whole + w
    inverse = 1.0 / whole
    weights = [w * inverse for w in weights]
    fill = TILE - HEADS * len(weights)
    columns = jnp.transpose(
        jnp.concatenate(weights + [jnp.zeros((fill, HD), jnp.float32)], axis=0)
    )
    for h in range(HEADS):
        cols = slice(h * HD, (h + 1) * HD)
        value = mine[:, cols] * columns[:, h : h + 1]
        for m in range(n_more):
            c = (m + 1) * HEADS + h
            value = value + travelled[m][:TILE, cols].astype(jnp.float32) * columns[:, c : c + 1]
        made[:, cols] = value.astype(made.dtype)
    copy = pltpu.make_async_copy(made, out.at[rows_of(at)], sem)
    copy.start()
    copy.wait()


def combine(at, parts, n_more, into=None):
    specs = [IN_VMEM] * len(parts)
    extra, aliases = [], {}
    if into is not None:
        specs.append(ANYWHERE)
        extra, aliases = [into], {len(parts): 0}
    return pl.pallas_call(
        functools.partial(combine_kernel, at, n_more),
        out_shape=jax.ShapeDtypeStruct((2 * TILE, HEADS * HD), jnp.bfloat16),
        in_specs=specs,
        out_specs=ANYWHERE,
        scratch_shapes=[
            pltpu.VMEM((TILE, HEADS * HD), jnp.bfloat16),
            pltpu.SemaphoreType.DMA,
        ],
        input_output_aliases=aliases,
        compiler_params=pltpu.CompilerParams(vmem_limit_bytes=VMEM),
        name="combine",
    )(*parts, *extra)


def local(query, key, value, live):
    n_uly, n_blk = lax.axis_size("uly"), lax.axis_size("blk")
    high = n_blk // TW

    def blk_move(block, pairs):
        return lax.ppermute(block, "blk", pairs)

    def uly_shift(block, distance):
        pairs = [(i, i + distance) for i in range(n_uly) if 0 <= i + distance < n_uly]
        return lax.ppermute(block, "uly", pairs)

    def uly_swap(block):
        return lax.ppermute(block, "uly", [(0, 1), (1, 0)])

    def halo(first, second):
        if is_small():
            return [uly_swap(first)]
        return [uly_shift(second, 1), uly_shift(first, -1)]

    mate_pairs = [(i, i ^ 1) for i in range(n_blk)]
    outer_pairs = [(i, i - 1) for i in range(0, n_blk, 2) if i % TW > 0]
    outer_pairs += [(i, i + 1) for i in range(1, n_blk, 2) if i % TW < TW - 1]

    if high == 2:
        swap = [(i, (i + TW) % n_blk) for i in range(n_blk)]
        beside = [(swap, swap, None)]
    else:
        down = [(i, i + TW) for i in range(n_blk - TW)]
        up = [(i + TW, i) for i in range(n_blk - TW)]
        beside = [(down, up, 1), (up, down, -1)]

    key, value = (pltpu.with_memory_space_constraint(a, pltpu.HBM) for a in (key, value))
    both, border, inner = pack(key, value)
    if is_small():
        far_live = blk_move(live, beside[0][0])
        far_live, query, both, border, inner = lax.optimization_barrier(
            (far_live, query, both, border, inner)
        )
        held = ((0, len(live), 0), (0, 0, 0), (0, 0, 0), (0, 0, 0))
        below = ((len(live), 0, 0), (0, 0, 0), (0, 0, 0), (0, 0, 0))
        live = lax.pad(live, 0, held) + lax.pad(far_live, 0, below)
        other_live = uly_swap(live)
        other_first = border
        border, other_live = lax.optimization_barrier((border, other_live))
        far_bias = [biases(1, None, (live, other_live), "bias_beside")]
        own_bias = biases(0, 0, (live, other_live), "bias_own")
    else:
        other_first = border
        own_live = lax.all_to_all(live, "uly", split_axis=1, concat_axis=0, tiled=True)
        own_bias = biases(0, 0, (own_live,), "bias_own")
        far_bias = [
            biases(1, height_step, (blk_move(own_live, there),), "bias_beside")
            for there, _, height_step in beside
        ]
    far_queries = [blk_move(query, there) for there, _, _ in beside]
    other_border = blk_move(other_first, outer_pairs)
    other_inner = blk_move(inner, outer_pairs)
    mate = blk_move(both, mate_pairs)
    own_halo = halo(border, inner)
    if is_small():
        other_border, far_bias = lax.optimization_barrier((other_border, far_bias))
    other_halo = halo(other_border, other_inner)

    def attend_beside(at, after):
        return [
            attend(at, bias, block, blocks, beyond, True, "attend_beside", after)
            for block, bias in zip(far_queries, far_bias)
        ]

    blocks, beyond = (both, mate, other_border, other_inner), []
    made = [None, None]
    after = []
    if is_small():
        made[1] = attend_beside(1, [])
        own_halo, after = lax.optimization_barrier((own_halo, made[1]))
    mate_halo = [blk_move(block, mate_pairs) for block in own_halo]
    beyond += [list(halos) for halos in zip(own_halo, mate_halo, other_halo)]
    if not is_small():
        made[1] = attend_beside(1, [])
    made[0] = attend_beside(0, after)
    returned = [
        [blk_move(part, back) for part, (_, back, _) in zip(made[at], beside)] for at in range(2)
    ]
    own = [
        attend(at, own_bias, query, blocks, beyond, False, "attend_own", [])
        for at in range(2)
    ]
    returned[1], own = lax.optimization_barrier((returned[1], own))
    out = None
    for at in (1, 0):
        out = combine(at, returned[at] + list(own[at]), len(beside), out)
    return out


def solution(mesh):
    return jax.shard_map(
        local,
        mesh=mesh,
        in_specs=(
            P(("uly", "blk"), None),
            P(("uly", "blk"), None),
            P(("uly", "blk"), None),
            P("uly", None, "blk", None),
        ),
        out_specs=P(("uly", "blk"), None),
        check_vma=False,
    )
```

```python
import functools

import jax
import jax.numpy as jnp
from jax import lax
from jax.experimental import pallas as pl
from jax.experimental.pallas import tpu as pltpu
from jax.sharding import PartitionSpec as P

HD = 128
HEADS = 8
TILE = 128
TW = 8
NEAR = 27
STEP = 4
COL = STEP * HD
C2 = HD ** (-0.5) * 1.4426950408889634
NONE = -1e30
STAT_ROWS = 8
TERMS = 3
CHUNK = 64
VMEM = 20 * 2**20

ANYWHERE = pl.BlockSpec(memory_space=pl.ANY)
IN_SMEM = pl.BlockSpec(memory_space=pltpu.SMEM)
IN_VMEM = pl.BlockSpec(memory_space=pltpu.VMEM)


def is_small():
    return lax.axis_size("uly") == 2 and lax.axis_size("blk") == 2 * TW


def frame_of(at):
    if is_small():
        g = lax.axis_index("uly")
        return 1 - g if at == 0 else g
    return at


def slots_of(at):
    if is_small():
        outward = 1 - 2 * lax.axis_index("uly")
        return ((0, 0), (1, -outward), (2, outward)) if at == 0 else ((0, outward), (1, 0))
    return ((0, 0), (1, 1), (2, -1)) if at == 0 else ((0, -1), (1, 0), (3, 1))


def rows_of(at):
    return pl.ds(pl.multiple_of(frame_of(at) * TILE, TILE), TILE)


def pack_kernel(key, value, both, border, inner, sems):
    loads = {}
    for row, (at, half, source) in enumerate(((1, 0, key), (0, 0, key), (0, 1, value), (1, 1, value))):
        to = both.at[pl.ds(row * TILE, TILE)]
        loads[at, half] = pltpu.make_async_copy(source.at[rows_of(at)], to, sems.at[row])
    for at in range(2):
        for half in range(2):
            loads[at, half].start()
    for half in range(2):
        loads[0, half].wait()
    border[...] = both[TILE : 3 * TILE]
    for half in range(2):
        loads[1, half].wait()
    inner[:TILE] = both[:TILE]
    inner[TILE:] = both[3 * TILE :]


def pack(key, value):
    def rows(tiles):
        return jax.ShapeDtypeStruct((tiles * TILE, HEADS * HD), key.dtype)

    return pl.pallas_call(
        pack_kernel,
        out_shape=(rows(4), rows(2), rows(2)),
        in_specs=[pl.BlockSpec(memory_space=pltpu.HBM)] * 2,
        out_specs=(IN_VMEM,) * 3,
        scratch_shapes=[pltpu.SemaphoreType.DMA((4,))],
        compiler_params=pltpu.CompilerParams(vmem_limit_bytes=VMEM),
        cost_estimate=pl.CostEstimate(flops=0, bytes_accessed=2**21, transcendentals=0),
        name="pack_kv",
    )(key, value)


def bias_kernel(which, height_step, n_live, *refs):
    live, out = refs[:n_live], refs[n_live]
    g, s = lax.axis_index("uly"), lax.axis_index("blk")
    height = 2 * (s // TW) - 1 if height_step is None else height_step
    width = 1 - 2 * (s % 2)

    def is_live(at, head, offset):
        if is_small():
            held = HEADS // 2
            place = (which * held + head % held, 2 * g + frame_of(at), 0, offset)
            return jnp.where(g == head // held, live[0][place], live[1][place]) > 0
        return live[0][head, frame_of(at), 0, offset] > 0

    for at in range(2):
        for slot, frame_step in slots_of(at):
            for c, width_step in enumerate((0, width, -width)):
                offset = 9 * (frame_step + 1) + 3 * (height + 1) + width_step + 1
                for head in range(HEADS):
                    row = bias_row(at, slot, c, head)
                    bias = jnp.where(is_live(at, head, offset), 0.0, NONE)
                    out[row : row + 1] = jnp.full((1, HD), bias, jnp.float32)


def bias_row(at, slot, c, head):
    counts = [len(slots_of(part)) for part in range(2)]
    order = [number for number, _ in slots_of(at)].index(slot)
    return ((counts[0] * HEADS if at else 0) + head * counts[at] + order) * 3 + c


def biases(which, height_step, live, name):
    rows = sum(len(slots_of(at)) for at in range(2)) * HEADS * 3
    return pl.pallas_call(
        functools.partial(bias_kernel, which, height_step, len(live)),
        out_shape=jax.ShapeDtypeStruct((rows, HD), jnp.float32),
        in_specs=[IN_SMEM] * len(live),
        out_specs=IN_VMEM,
        compiler_params=pltpu.CompilerParams(vmem_limit_bytes=VMEM),
        name=name,
    )(*live)


def attend_kernel(at, places, travels, bias, query, *refs):
    out, stats_out = (refs[-1], None) if travels else refs[-2:]
    rows = rows_of(at)
    lane = lax.broadcasted_iota(jnp.int32, (TILE, HD), 1)

    cols = [slice(h * HD, (h + 1) * HD) for h in range(HEADS)]
    for step in range(HEADS // STEP):
        heads = range(step * STEP, (step + 1) * STEP)
        scores, highest = {}, {}
        for h in heads:
            q = query[rows, cols[h]]
            for block, (k_row, _, tiles) in enumerate(places):
                keys = refs[block][k_row : k_row + len(tiles) * TILE, cols[h]]
                score = lax.dot_general(
                    q, keys, (((1,), (1,)), ((), ())), preferred_element_type=jnp.float32
                )
                for i, t in enumerate(tiles):
                    part = score[:, i * TILE : (i + 1) * TILE]
                    row = bias_row(at, *t, h)
                    part = part + bias[row : row + 1]
                    scores[h, t] = part
                    highest[h] = jnp.maximum(highest[h], part) if h in highest else part
        top = {h: jnp.max(highest[h], axis=1, keepdims=True) for h in heads}
        shift = {h: top[h] * C2 for h in heads}
        mixed, sums = {}, {}
        for h in heads:
            for block, (_, v_row, tiles) in enumerate(places):
                weights = []
                for t in reversed(tiles):
                    w = jnp.exp2(scores[h, t] * C2 - shift[h])
                    sums[h] = sums[h] + w if h in sums else w
                    weights.append(w.astype(jnp.bfloat16))
                values = refs[block][v_row : v_row + len(tiles) * TILE, cols[h]]
                o = jnp.dot(
                    weights[0] if len(weights) == 1 else jnp.concatenate(weights, axis=1),
                    values,
                    preferred_element_type=jnp.float32,
                )
                mixed[h] = mixed[h] + o if h in mixed else o
        total = {h: jnp.sum(sums[h], axis=1, keepdims=True) for h in heads}
        stats = jnp.zeros((TILE, HD), jnp.float32)
        for i, h in enumerate(heads):
            if travels:
                any_live = top[h] > 0.5 * NONE
                total[h] = jnp.where(any_live, total[h], 0.0)
                mixed[h] = mixed[h] * jnp.where(any_live, 1.0 / total[h], 0.0)
            out[:TILE, cols[h]] = mixed[h].astype(out.dtype)
            stats = jnp.where(lane == i, top[h], stats)
            stats = jnp.where(lane == STEP + i, total[h], stats)
        stats = jnp.transpose(stats)[:STAT_ROWS]
        if travels:
            for term in range(TERMS):
                rounded = stats.astype(jnp.bfloat16)
                out[TILE:, cols[heads[term]]] = rounded
                stats = stats - rounded.astype(jnp.float32)
            out[TILE:, cols[heads[TERMS]]] = jnp.zeros((STAT_ROWS, HD), jnp.bfloat16)
        else:
            stats_out[step * STAT_ROWS : (step + 1) * STAT_ROWS] = stats


def attend(at, bias, query, both, beyond, travels, name, after):
    blocks = list(both)
    places = [(0, 2 * TILE, ((1, c), (0, c))) for c in range(2)]
    places += [(0, TILE, ((slot, 2),)) for slot in range(2)]
    for slot, _ in slots_of(at)[2:]:
        blocks += beyond[slot - 2]
        places += [(0, TILE, ((slot, c),)) for c in range(3)]
    pairs = sum(len(tiles) for _, _, tiles in places) * HEADS
    steps = HEADS // STEP
    if travels:
        out_shape = jax.ShapeDtypeStruct((TILE + STAT_ROWS, HEADS * HD), jnp.bfloat16)
    else:
        out_shape = (
            jax.ShapeDtypeStruct((TILE, HEADS * HD), jnp.float32),
            jax.ShapeDtypeStruct((steps * STAT_ROWS, HD), jnp.float32),
        )
    return pl.pallas_call(
        functools.partial(attend_kernel, at, places, travels),
        out_shape=out_shape,
        in_specs=[IN_VMEM] * (2 + len(blocks)) + [ANYWHERE] * len(after),
        out_specs=IN_VMEM if travels else (IN_VMEM, IN_VMEM),
        compiler_params=pltpu.CompilerParams(vmem_limit_bytes=VMEM),
        cost_estimate=pl.CostEstimate(
            flops=4 * pairs * TILE * TILE * HD,
            bytes_accessed=(pairs // HEADS + 2) * 2 * TILE * HEADS * HD * 2,
            transcendentals=pairs * TILE * TILE,
        ),
        name=name,
    )(bias, query, *blocks, *after)


def split_stats(per_step):
    tops = jnp.concatenate([stats[:STEP] for stats in per_step], axis=0)
    totals = jnp.concatenate([stats[STEP : 2 * STEP] for stats in per_step], axis=0)
    return tops, totals


def own_stats(ref):
    steps = range(HEADS // STEP)
    return split_stats([ref[step * STAT_ROWS : (step + 1) * STAT_ROWS] for step in steps])


def travelled_stats(ref):
    per_step = []
    for step in range(HEADS // STEP):
        first = step * COL
        terms = [ref[TILE:, first + HD * t : first + HD * (t + 1)] for t in range(TERMS)]
        per_step.append(sum(term.astype(jnp.float32) for term in terms))
    return split_stats(per_step)


def combine_kernel(at, n_more, *refs):
    out, made, sems = refs[-3:]
    travelled, (mine, stats) = refs[:n_more], refs[n_more : n_more + 2]
    top, total = own_stats(stats)
    more = []
    best = top
    for m in range(n_more):
        top2, total2 = travelled_stats(travelled[m])
        top2 = jnp.where(total2 > 0.0, top2, NONE)
        more.append((top2, total2))
        best = jnp.maximum(best, top2)
    own = jnp.exp2((top - best) * C2)
    weights = [own]
    whole = total * own
    for top2, total2 in more:
        w = jnp.exp2((top2 - best) * C2) * total2
        weights.append(w)
        whole = whole + w
    inverse = 1.0 / whole
    weights = [w * inverse for w in weights]
    fill = TILE - HEADS * len(weights)
    columns = jnp.transpose(
        jnp.concatenate(weights + [jnp.zeros((fill, HD), jnp.float32)], axis=0)
    )
    begin = frame_of(at) * TILE
    copies = []
    for first in range(0, TILE, CHUNK):
        rows = slice(first, first + CHUNK)
        for h in range(HEADS):
            cols = slice(h * HD, (h + 1) * HD)
            value = mine[rows, cols] * columns[rows, h : h + 1]
            for m in range(n_more):
                c = (m + 1) * HEADS + h
                part = travelled[m][rows, cols].astype(jnp.float32)
                value = value + part * columns[rows, c : c + 1]
            made[rows, cols] = value.astype(made.dtype)
        to = out.at[pl.ds(pl.multiple_of(begin + first, CHUNK), CHUNK)]
        copies.append(pltpu.make_async_copy(made.at[rows], to, sems.at[first // CHUNK]))
        copies[-1].start()
    for copy in copies:
        copy.wait()


def combine(at, parts, n_more, into=None):
    specs = [IN_VMEM] * len(parts)
    extra, aliases = [], {}
    if into is not None:
        specs.append(ANYWHERE)
        extra, aliases = [into], {len(parts): 0}
    return pl.pallas_call(
        functools.partial(combine_kernel, at, n_more),
        out_shape=jax.ShapeDtypeStruct((2 * TILE, HEADS * HD), jnp.bfloat16),
        in_specs=specs,
        out_specs=ANYWHERE,
        scratch_shapes=[
            pltpu.VMEM((TILE, HEADS * HD), jnp.bfloat16),
            pltpu.SemaphoreType.DMA((TILE // CHUNK,)),
        ],
        input_output_aliases=aliases,
        compiler_params=pltpu.CompilerParams(vmem_limit_bytes=VMEM),
        name="combine",
    )(*parts, *extra)


def local(query, key, value, live):
    n_uly, n_blk = lax.axis_size("uly"), lax.axis_size("blk")
    high = n_blk // TW

    def blk_move(block, pairs):
        return lax.ppermute(block, "blk", pairs)

    def uly_shift(block, distance):
        pairs = [(i, i + distance) for i in range(n_uly) if 0 <= i + distance < n_uly]
        return lax.ppermute(block, "uly", pairs)

    def uly_swap(block):
        return lax.ppermute(block, "uly", [(0, 1), (1, 0)])

    def halo(first, second):
        if is_small():
            return [uly_swap(first)]
        return [uly_shift(second, 1), uly_shift(first, -1)]

    mate_pairs = [(i, i ^ 1) for i in range(n_blk)]
    outer_pairs = [(i, i - 1) for i in range(0, n_blk, 2) if i % TW > 0]
    outer_pairs += [(i, i + 1) for i in range(1, n_blk, 2) if i % TW < TW - 1]

    if high == 2:
        swap = [(i, (i + TW) % n_blk) for i in range(n_blk)]
        beside = [(swap, swap, None)]
    else:
        down = [(i, i + TW) for i in range(n_blk - TW)]
        up = [(i + TW, i) for i in range(n_blk - TW)]
        beside = [(down, up, 1), (up, down, -1)]

    key, value = (pltpu.with_memory_space_constraint(a, pltpu.HBM) for a in (key, value))
    both, border, inner = pack(key, value)
    if is_small():
        far_live = blk_move(live, beside[0][0])
        far_live, query, both, border, inner = lax.optimization_barrier(
            (far_live, query, both, border, inner)
        )
        held = ((0, len(live), 0), (0, 0, 0), (0, 0, 0), (0, 0, 0))
        below = ((len(live), 0, 0), (0, 0, 0), (0, 0, 0), (0, 0, 0))
        live = lax.pad(live, 0, held) + lax.pad(far_live, 0, below)
        other_live = uly_swap(live)
        other_first = border
        border, other_live = lax.optimization_barrier((border, other_live))
        far_bias = [biases(1, None, (live, other_live), "bias_beside")]
        own_bias = biases(0, 0, (live, other_live), "bias_own")
    else:
        other_first = border
        own_live = lax.all_to_all(live, "uly", split_axis=1, concat_axis=0, tiled=True)
        own_bias = biases(0, 0, (own_live,), "bias_own")
        far_bias = [
            biases(1, height_step, (blk_move(own_live, there),), "bias_beside")
            for there, _, height_step in beside
        ]
    far_queries = [blk_move(query, there) for there, _, _ in beside]
    other_border = blk_move(other_first, outer_pairs)
    other_inner = blk_move(inner, outer_pairs)
    mate = blk_move(both, mate_pairs)
    own_halo = halo(border, inner)
    if is_small():
        other_border, far_bias = lax.optimization_barrier((other_border, far_bias))
        token = blk_move(other_border[:TILE], mate_pairs)
        other_border, token = lax.optimization_barrier((other_border, token))
    other_halo = halo(other_border, other_inner)

    def attend_beside(at, after):
        return [
            attend(at, bias, block, blocks, beyond, True, "attend_beside", after)
            for block, bias in zip(far_queries, far_bias)
        ]

    blocks, beyond = (both, mate, other_border, other_inner), []
    made = [None, None]
    after = []
    if is_small():
        made[1] = attend_beside(1, [])
        own_halo, after = lax.optimization_barrier((own_halo, made[1]))
        after = after + [token]
    mate_halo = [blk_move(block, mate_pairs) for block in own_halo]
    beyond += [list(halos) for halos in zip(own_halo, mate_halo, other_halo)]
    if not is_small():
        made[1] = attend_beside(1, [])
    made[0] = attend_beside(0, after)
    returned = [
        [blk_move(part, back) for part, (_, back, _) in zip(made[at], beside)] for at in range(2)
    ]
    own = [
        attend(at, own_bias, query, blocks, beyond, False, "attend_own", [])
        for at in range(2)
    ]
    returned[1], own = lax.optimization_barrier((returned[1], own))
    out = None
    for at in (1, 0):
        out = combine(at, returned[at] + list(own[at]), len(beside), out)
    return out


def solution(mesh):
    return jax.shard_map(
        local,
        mesh=mesh,
        in_specs=(
            P(("uly", "blk"), None),
            P(("uly", "blk"), None),
            P(("uly", "blk"), None),
            P("uly", None, "blk", None),
        ),
        out_specs=P(("uly", "blk"), None),
        check_vma=False,
    )
```
